128 devices in a mesh: rows: 16 (over y, x), inner: 8 (over z, core).
Axes of the slice: x: 4, y: 4, z: 4, core: 2. Of those that a mesh axis runs over, the one named last changes fastest.
Arguments:
- activations: bfloat16 [131072, 8192], P(('rows', 'inner')), may hold values from -128 to 128
- sketch_matrix: bfloat16 [8192, 256], replicated, may hold values from -0.0625 to 0.0625
- row_counts: int32 [128], P(('rows', 'inner')), may hold values from 512 to 1024, as said below
Outputs:
- basis: float32 [131072, 256], P(('rows', 'inner'))
- projected: float32 [8192, 256], P('rows')
The draws below stay inside these ranges and needn't reach their ends.
Inputs may be any that keep to these rules, and one draw needn't show every extreme that they name: `row_counts`: some device has all 1024 slots live.
All inputs are finite; a program needn't handle non-finite values.
Results may differ from the reference program's by a relative error of at most 0.0003.
Values sent between devices are 32-bit elements; how exact they have to be, the bound alone decides.
No kernel may reach another device: no remote copies, remote signals or barrier semaphores. Data moves between devices by JAX's collectives and lax.ppermute only.
A program may use at most 128 MiB of HBM per device.

```python
import math
import jax
import jax.numpy as jnp
from jax import lax

D = 8192
K = 256
ROWS_DEV = 1024
TOKENS = 131072
N_ROWS = 16
N_INNER = 8


def draw_activations(key, part):
    key = jax.random.fold_in(key, 2)
    first, second = jax.random.split(key, 2)
    position = jnp.arange(TOKENS, dtype=jnp.float32) / TOKENS
    rising = jnp.exp(jnp.log(3.0) * position)
    spread = jnp.exp(jax.random.uniform(first, (TOKENS,), jnp.float32) * jnp.log(10.0))
    entries = jnp.clip(jax.random.normal(second, (TOKENS, D), jnp.float32), -4.0, 4.0)
    values = entries * (rising * spread)[:, None]
    return values.astype(jnp.bfloat16)


def draw_row_counts(key, part):
    key = jax.random.fold_in(key, 1)
    first, second = jax.random.split(key)
    devices = N_ROWS * N_INNER
    values = jax.random.randint(first, (devices,), ROWS_DEV // 2, ROWS_DEV + 1)
    chosen = jax.random.randint(second, (), 0, devices)
    return values.at[chosen].set(ROWS_DEV).astype(jnp.int32)


def centred(stream_key, dims, deviation, limit, kind=jnp.bfloat16):
    return jnp.clip(deviation * jax.random.normal(stream_key, dims, jnp.float32), -limit, limit).astype(kind)


def setup_inputs(seed: int = 0) -> dict:
    keys = jax.random.split(jax.random.key(seed), 4)
    activations = draw_activations(jax.random.fold_in(keys[3], 71), 0)
    sketch_matrix = centred(keys[1], (D, K), D ** -0.5, 0.0625)
    row_counts = draw_row_counts(jax.random.fold_in(keys[3], 71), 0)
    return {"activations": activations, "sketch_matrix": sketch_matrix, "row_counts": row_counts}


def reference(activations, sketch_matrix, row_counts):
    devices = N_ROWS * N_INNER
    blocks = activations.reshape(devices, ROWS_DEV, D)
    slots = lax.iota(jnp.int32, ROWS_DEV)

    def masking(block, count):
        live = (slots < count)[:, None]
        return jnp.where(live, block, jnp.zeros_like(block))

    def gram_step(total, item):
        block, count = item
        masked = masking(block, count)
        sketch = jnp.dot(masked.astype(jnp.float32), sketch_matrix.astype(jnp.float32), preferred_element_type=jnp.float32)
        total = total + jnp.dot(sketch.T, sketch, precision=lax.Precision.HIGHEST)
        return (total, sketch)
    gram, sketches = lax.scan(gram_step, jnp.zeros((K, K), jnp.float32), (blocks, row_counts))
    lower = jnp.linalg.cholesky(gram)
    factor = jax.scipy.linalg.solve_triangular(lower, sketches.reshape(TOKENS, K).T, lower=True).T
    factors = factor.reshape(devices, ROWS_DEV, K)

    def project_step(total, item):
        block, count, piece = item
        masked = masking(block, count).astype(jnp.float32)
        return (total + jnp.dot(masked.T, piece, precision=lax.Precision.HIGHEST), 0)
    summed, unused = lax.scan(project_step, jnp.zeros((D, K), jnp.float32), (blocks, row_counts, factors))
    basis = factor * math.sqrt(TOKENS)
    projected = summed * math.sqrt(D / TOKENS)
    return (basis, projected)
```

```python
import math

import jax
import jax.numpy as jnp
from jax import lax
from jax.experimental import pallas as pl
from jax.experimental.pallas import tpu as pltpu
from jax.sharding import PartitionSpec as P

SIDE = 4
BOTH = ("rows", "inner")
F32 = jnp.float32
BF16 = jnp.bfloat16
HIGH = lax.Precision.HIGHEST
NT = (((1,), (1,)), ((), ()))
DEPTH = 1024
WIDE = 256


def device(y, x, z, core):
    return ((y % SIDE) * SIDE + x % SIDE) * 2 * SIDE + (z % SIDE) * 2 + core


def pairs(move):
    found = []
    for y in range(SIDE):
        for x in range(SIDE):
            for z in range(SIDE):
                for core in range(2):
                    found.append((device(y, x, z, core), device(*move(y, x, z, core))))
    return found


def step_on(axis, steps, y, x, z, core):
    return (y + steps * (axis == "y"), x + steps * (axis == "x"), z + steps * (axis == "z"), core)


def send(value, axes, steps):
    return lax.ppermute(value, BOTH, pairs(lambda y, x, z, core: step_on(axes[core], steps, y, x, z, core)))


def swap_cores(value):
    return lax.ppermute(value, BOTH, pairs(lambda y, x, z, core: (y, x, z, 1 - core)))


def sum_axis(value, axes):
    one, two, three = (send(value, axes, steps) for steps in (1, 2, 3))
    return (value + two) + (one + three)


def sketch_kernel(place, count, act, test, sketch, split, gram_mine, gram_other, total):
    step = pl.program_id(0)
    part = jnp.dot(act[...], test[...], preferred_element_type=F32)

    @pl.when(step == 0)
    def _():
        total[...] = part

    @pl.when(step > 0)
    def _():
        total[...] += part

    @pl.when(step == pl.num_programs(0) - 1)
    def _():
        rows, columns = total.shape
        half = columns // 2
        gram = jnp.zeros((columns, columns), F32)
        for first in range(0, rows, 256):
            here = pl.ds(first, 256)
            slots = lax.broadcasted_iota(jnp.int32, (256, columns), 0) + first
            live = jnp.where(slots < count[0], total[here, :], 0.0)
            sketch[here, :] = live
            turned = live.T
            high = turned.astype(BF16)
            split[:columns, here] = high
            split[columns:, here] = (turned - high.astype(F32)).astype(BF16)
            gram += lax.dot_general(turned, turned, NT, precision=HIGH, preferred_element_type=F32)
        core = place[4]
        upper = jnp.concatenate([gram[:half, :half], gram[: half // 2, half:]], 0)
        lower = jnp.concatenate([gram[half:, half:], gram[half // 2 : half, half:]], 0)
        gram_mine[...] = jnp.where(core == 0, upper, lower)
        gram_other[...] = jnp.where(core == 0, lower, upper)


def sketch_call(place, count, activations, sketch_matrix):
    rows, width = activations.shape
    columns = sketch_matrix.shape[1]
    packed = (columns // 2 + columns // 4, columns // 2)
    whole = lambda step, *_: (0, 0)
    return pl.pallas_call(
        sketch_kernel,
        out_shape=[
            jax.ShapeDtypeStruct((rows, columns), F32),
            jax.ShapeDtypeStruct((2 * columns, rows), BF16),
            jax.ShapeDtypeStruct(packed, F32),
            jax.ShapeDtypeStruct(packed, F32),
        ],
        grid_spec=pltpu.PrefetchScalarGridSpec(
            num_scalar_prefetch=2,
            grid=(width // DEPTH,),
            in_specs=[
                pl.BlockSpec((rows, DEPTH), lambda step, *_: (0, step)),
                pl.BlockSpec((DEPTH, columns), lambda step, *_: (step, 0)),
            ],
            out_specs=[
                pl.BlockSpec((rows, columns), whole),
                pl.BlockSpec((2 * columns, rows), whole),
                pl.BlockSpec(packed, whole),
                pl.BlockSpec(packed, whole),
            ],
            scratch_shapes=[pltpu.VMEM((rows, columns), F32)],
        ),
        compiler_params=pltpu.CompilerParams(vmem_limit_bytes=40 * 2**20),
        cost_estimate=pl.CostEstimate(
            flops=2 * rows * width * columns, bytes_accessed=2 * width * (rows + columns), transcendentals=0
        ),
        name="sketch",
    )(place, count, activations, sketch_matrix)


def projection_kernel(adds, place, split, act, *refs):
    columns = split.shape[0] // 2
    both = jnp.dot(split[...], act[...], preferred_element_type=F32)
    block = both[:columns] + both[columns:]
    if adds:
        block += refs[0][0, 0]
        first, second = refs[1:]

        @pl.when(pl.program_id(0) == 0)
        def _():
            first[0] = block

        @pl.when(pl.program_id(0) == 1)
        def _():
            second[0] = block
    else:
        refs[0][0, 0] = block


def projection_call(place, split, activations, offsets, other, received=None):
    rows, width = activations.shape
    columns = split.shape[0] // 2
    one, two = offsets

    def act_map(i, j, place):
        steps = jnp.where(i == 0, one, two)
        core = place[4] + other
        core = jnp.where(core == 2, 0, core)
        y = place[0] + jnp.where(core == 0, j, steps)
        x = place[1] + jnp.where(core == 0, steps, j)
        return (0, ((y % SIDE) * SIDE + x % SIDE) * 2 + core)

    both = pl.BlockSpec((1, 1, columns, WIDE), lambda i, j, *_: (i, j, 0, 0))
    block = (1, columns, WIDE)
    in_specs = [
        pl.BlockSpec((2 * columns, rows), lambda i, j, *_: (0, 0)),
        pl.BlockSpec((rows, WIDE), act_map),
    ]
    operands = [place, split, activations]
    if received is None:
        out_shape = jax.ShapeDtypeStruct((2, SIDE, columns, WIDE), F32)
        out_specs = both
    else:
        in_specs.append(both)
        operands.append(received)
        out_shape = [jax.ShapeDtypeStruct((SIDE, columns, WIDE), F32)] * 2
        out_specs = [
            pl.BlockSpec(block, lambda i, j, *_: (jnp.where(i == 0, j, SIDE - 1), 0, 0)),
            pl.BlockSpec(block, lambda i, j, *_: (jnp.where(i == 0, 0, j), 0, 0)),
        ]
    blocks = 2 * SIDE
    return pl.pallas_call(
        lambda *refs: projection_kernel(received is not None, *refs),
        out_shape=out_shape,
        grid_spec=pltpu.PrefetchScalarGridSpec(
            num_scalar_prefetch=1, grid=(2, SIDE), in_specs=in_specs, out_specs=out_specs
        ),
        compiler_params=pltpu.CompilerParams(vmem_limit_bytes=20 * 2**20),
        cost_estimate=pl.CostEstimate(
            flops=4 * blocks * rows * WIDE * columns,
            bytes_accessed=blocks * (2 * WIDE * rows + 8 * WIDE * columns),
            transcendentals=0,
        ),
        name="projection",
    )(*operands)


def on_device(activations, sketch_matrix, row_counts):
    rows_here, width = activations.shape
    columns = sketch_matrix.shape[1]
    half = columns // 2
    total_rows = rows_here * lax.axis_size(BOTH)
    row, inner = lax.axis_index("rows"), lax.axis_index("inner")
    core = inner % 2
    place = jnp.stack([row // SIDE, row % SIDE, inner // 2, inner, core]).astype(jnp.int32)

    sketch, split, gram_mine, gram_other = sketch_call(place, row_counts, activations, sketch_matrix)

    packed = gram_mine + swap_cores(gram_other)
    far_a = projection_call(place, split, activations, (1, 3), 1)
    near_a = swap_cores(far_a)
    packed = sum_axis(packed, ("z", "x"))
    far_b = projection_call(place, split, activations, (2, 0), 1)
    near_b = swap_cores(far_b)
    to_one, to_three = projection_call(place, split, activations, (1, 3), 0, near_a)
    one = send(to_one, ("x", "y"), 1)
    three = send(to_three, ("x", "y"), 3)
    to_two, mine = projection_call(place, split, activations, (2, 0), 0, near_b)
    two = send(to_two, ("x", "y"), 2)
    packed = sum_axis(packed, ("x", "y"))
    packed = sum_axis(packed, ("y", "z"))
    swapped = swap_cores(packed)
    upper = jnp.where(core == 0, packed, swapped)
    lower = jnp.where(core == 0, swapped, packed)
    corner = jnp.concatenate([upper[half:], lower[half:]], 0)
    gram = jnp.concatenate(
        [
            jnp.concatenate([upper[:half], corner], 1),
            jnp.concatenate([corner.T, lower[:half]], 1),
        ],
        0,
    )

    blocks = [(mine[j] + two[j]) + (one[j] + three[j]) for j in range(SIDE)]
    arrived = [None] + [send(blocks[j], ("y", "x"), j) for j in range(1, SIDE)]
    block = (blocks[0] + arrived[2]) + (arrived[1] + arrived[3])
    block = sum_axis(block, ("z", "z"))
    other_block = swap_cores(block)

    factor_lower = jnp.linalg.cholesky(gram)
    inverse = jax.scipy.linalg.solve_triangular(factor_lower, jnp.eye(columns, dtype=F32), lower=True)
    basis = lax.dot_general(sketch, inverse * math.sqrt(total_rows), NT, precision=HIGH)
    turned = jnp.where(
        core == 0, jnp.concatenate([block, other_block], 1), jnp.concatenate([other_block, block], 1)
    )
    projected = lax.dot_general(
        turned, inverse * math.sqrt(width / total_rows), (((0,), (1,)), ((), ())), precision=HIGH
    )
    return (basis, projected)


def solution(mesh):
    return jax.shard_map(
        on_device,
        mesh=mesh,
        in_specs=(P(("rows", "inner"), None), P(), P(("rows", "inner"))),
        out_specs=(P(("rows", "inner"), None), P("rows", None)),
        check_vma=False,
    )
```

```python
import math

import jax
import jax.numpy as jnp
from jax import lax
from jax.experimental import pallas as pl
from jax.experimental.pallas import tpu as pltpu
from jax.sharding import PartitionSpec as P

SIDE = 4
BOTH = ("rows", "inner")
F32 = jnp.float32
BF16 = jnp.bfloat16
HIGH = lax.Precision.HIGHEST
NT = (((1,), (1,)), ((), ()))
TN = (((0,), (0,)), ((), ()))
GROUP = 8
PANEL = 64
AHEAD = 2
DEPTH = 1024
WIDE = 256


def device(y, x, z, core):
    return ((y % SIDE) * SIDE + x % SIDE) * 2 * SIDE + (z % SIDE) * 2 + core


def pairs(move):
    found = []
    for y in range(SIDE):
        for x in range(SIDE):
            for z in range(SIDE):
                for core in range(2):
                    found.append((device(y, x, z, core), device(*move(y, x, z, core))))
    return found


def step_on(axis, steps, y, x, z, core):
    return (y + steps * (axis == "y"), x + steps * (axis == "x"), z + steps * (axis == "z"), core)


def send(value, axes, steps):
    return lax.ppermute(value, BOTH, pairs(lambda y, x, z, core: step_on(axes[core], steps, y, x, z, core)))


def swap_cores(value):
    return lax.ppermute(value, BOTH, pairs(lambda y, x, z, core: (y, x, z, 1 - core)))


def pair_axis(value, axes):
    for partner in (lambda i: i ^ 1, lambda i: SIDE - 1 - i):

        def move(y, x, z, core):
            at = {"y": y, "x": x, "z": z}
            at[axes[core]] = partner(at[axes[core]])
            return (at["y"], at["x"], at["z"], core)

        value = value + lax.ppermute(value, BOTH, pairs(move))
    return value


def sketch_kernel(place, count, act, test, held, sketch, split, gram_mine, gram_other, tests, act_sems, test_sems):
    rows, width = held.shape
    columns = sketch.shape[1]
    half = columns // 2
    copies = []
    for step in range(width // DEPTH):
        part = pl.ds(step * DEPTH, DEPTH)
        copies.append(
            (
                pltpu.make_async_copy(test.at[part, :], tests.at[part, :], test_sems.at[step]),
                pltpu.make_async_copy(act.at[:, part], held.at[:, part], act_sems.at[step]),
            )
        )
    for pair in copies[:AHEAD]:
        for copy in pair:
            copy.start()
    for step, pair in enumerate(copies):
        for copy in pair:
            copy.wait()
        for copy in copies[step + AHEAD] if step + AHEAD < len(copies) else ():
            copy.start()
        part = pl.ds(step * DEPTH, DEPTH)
        product = jnp.dot(held[:, part], tests[part, :], preferred_element_type=F32)
        if step == 0:
            sketch[...] = product
        else:
            sketch[...] += product
    gram = jnp.zeros((columns, columns), F32)
    for first in range(0, rows, 256):
        here = pl.ds(first, 256)
        slots = lax.broadcasted_iota(jnp.int32, (256, columns), 0) + first
        live = jnp.where(slots < count[0], sketch[here, :], 0.0)
        sketch[here, :] = live
        turned = live.T
        high = turned.astype(BF16)
        split[:columns, here] = high
        split[columns:, here] = (turned - high.astype(F32)).astype(BF16)
        gram += lax.dot_general(turned, turned, NT, precision=HIGH, preferred_element_type=F32)
    core = place[4]
    upper = jnp.concatenate([gram[:half, :half], gram[: half // 2, half:]], 0)
    lower = jnp.concatenate([gram[half:, half:], gram[half // 2 : half, half:]], 0)
    gram_mine[...] = jnp.where(core == 0, upper, lower)
    gram_other[...] = jnp.where(core == 0, lower, upper)


def sketch_call(place, count, activations, sketch_matrix):
    rows, width = activations.shape
    columns = sketch_matrix.shape[1]
    packed = (columns // 2 + columns // 4, columns // 2)
    steps = width // DEPTH
    smem, anywhere, vmem = (pl.BlockSpec(memory_space=space) for space in (pltpu.SMEM, pltpu.HBM, pltpu.VMEM))
    return pl.pallas_call(
        sketch_kernel,
        out_shape=[
            pltpu.VMEM((rows, width), BF16),
            pltpu.VMEM((rows, columns), F32),
            pltpu.VMEM((2 * columns, rows), BF16),
            pltpu.VMEM(packed, F32),
            pltpu.VMEM(packed, F32),
        ],
        in_specs=[smem, smem, anywhere, anywhere],
        out_specs=[vmem] * 5,
        scratch_shapes=[
            pltpu.VMEM((width, columns), BF16),
            pltpu.SemaphoreType.DMA((steps,)),
            pltpu.SemaphoreType.DMA((steps,)),
        ],
        compiler_params=pltpu.CompilerParams(vmem_limit_bytes=12 * 2**20),
        cost_estimate=pl.CostEstimate(
            flops=2 * rows * width * columns, bytes_accessed=2 * width * (rows + columns), transcendentals=0
        ),
        name="sketch",
    )(place, count, *(pltpu.with_memory_space_constraint(value, pltpu.HBM) for value in (activations, sketch_matrix)))


def projection_kernel(offsets, other, place, split, held, *refs):
    columns = split.shape[0] // 2
    core = place[4] + other
    core = jnp.where(core == 2, 0, core)
    for i, steps in enumerate(offsets):
        for j in range(SIDE):
            y = (place[0] + jnp.where(core == 0, j, steps)) % SIDE
            x = (place[1] + jnp.where(core == 0, steps, j)) % SIDE
            first = pl.multiple_of(((y * SIDE + x) * 2 + core) * WIDE, WIDE)
            both = jnp.dot(split[...], held[:, pl.ds(first, WIDE)], preferred_element_type=F32)
            block = both[:columns] + both[columns:]
            if other:
                refs[0][i, j] = block
            else:
                refs[1 + i][j] = block + refs[0][i, j]


def projection_call(place, split, held, offsets, other, received=None):
    rows = held.shape[0]
    columns = split.shape[0] // 2
    smem, vmem = (pl.BlockSpec(memory_space=space) for space in (pltpu.SMEM, pltpu.VMEM))
    in_specs = [smem, vmem, vmem]
    operands = [place, split, held]
    if other:
        out_shape = pltpu.VMEM((2, SIDE, columns, WIDE), F32)
        out_specs = vmem
    else:
        in_specs.append(vmem)
        operands.append(received)
        out_shape = [pltpu.VMEM((SIDE, columns, WIDE), F32)] * 2
        out_specs = [vmem] * 2
    blocks = 2 * SIDE
    return pl.pallas_call(
        lambda *refs: projection_kernel(offsets, other, *refs),
        out_shape=out_shape,
        in_specs=in_specs,
        out_specs=out_specs,
        compiler_params=pltpu.CompilerParams(vmem_limit_bytes=8 * 2**20),
        cost_estimate=pl.CostEstimate(
            flops=4 * blocks * rows * WIDE * columns,
            bytes_accessed=blocks * 8 * WIDE * columns,
            transcendentals=0,
        ),
        name="projection",
    )(*operands)


def small_inverse(matrix):
    size = matrix.shape[0]
    groups = [matrix[first : first + GROUP, :] for first in range(0, size, GROUP)]
    lane = lax.broadcasted_iota(jnp.int32, (1, size), 1)
    sublane = lax.broadcasted_iota(jnp.int32, (GROUP, size), 0)
    for at in range(len(groups)):
        first = GROUP * at
        inside = (lane >= first) & (lane < first + GROUP)
        columns = [
            [jnp.broadcast_to(group[:, first + j : first + j + 1], (GROUP, size)) for j in range(GROUP)]
            for group in groups[at:]
        ]
        top = columns[0]
        scaled, done = [], []
        for j in range(GROUP):
            pivot = top[j][j : j + 1, :]
            reciprocal = 1.0 / pivot
            factors = [top[k][j : j + 1, :] * reciprocal for k in range(j + 1, GROUP)]
            for column in columns:
                for k, factor in enumerate(factors, j + 1):
                    column[k] = column[k] - column[j] * factor
            row = jnp.where(inside, 0.0, groups[at][j : j + 1, :])
            for i in range(j):
                row = row - top[i][j : j + 1, :] * scaled[i]
            row = jnp.where(lane == first + j, 1.0, row)
            scaled.append(row * reciprocal)
            done.append(row * lax.rsqrt(pivot))
        for below, column in enumerate(columns[1:], at + 1):
            rest = jnp.where(inside, 0.0, groups[below])
            for j in range(GROUP):
                rest = rest - column[j] * scaled[j]
            groups[below] = rest
        for j in range(GROUP):
            groups[at] = jnp.where(sublane == j, done[j], groups[at])
    rows, cols = (lax.broadcasted_iota(jnp.int32, (size, size), axis) for axis in (0, 1))
    return jnp.where(rows >= cols, jnp.concatenate(groups, 0), 0.0)


def inverse_kernel(place, mine, other, inverse, work):
    size = work.shape[0]
    half = size // 2
    core = place[4]
    upper = jnp.where(core == 0, mine[...], other[...])
    lower = jnp.where(core == 0, other[...], mine[...])
    corner = jnp.concatenate([upper[half:], lower[half:]], 0)
    work[:half, :half] = upper[:half]
    work[:half, half:] = corner
    work[half:, :half] = corner.T
    work[half:, half:] = lower[:half]
    for first in range(0, size, PANEL):
        past = first + PANEL
        rows = pl.ds(first, PANEL)
        block = small_inverse(work[rows, first:past])
        lane = lax.broadcasted_iota(jnp.int32, (PANEL, size), 1)
        parts = [jnp.zeros((PANEL, first), F32)] * (first > 0) + [block]
        parts += [jnp.zeros((PANEL, size - past), F32)] * (past < size)
        placed = jnp.concatenate(parts, 1) if len(parts) > 1 else block
        panel = jnp.dot(block, work[rows, :], precision=HIGH, preferred_element_type=F32)
        panel = jnp.where((lane >= first) & (lane < past), placed, panel)
        inverse[rows, :] = jnp.where(lane < past, panel, 0.0)
        if past < size:
            update = lax.dot_general(panel[:, past:], panel, TN, precision=HIGH, preferred_element_type=F32)
            lane = lax.broadcasted_iota(jnp.int32, (size - past, size), 1)
            old = jnp.where((lane >= first) & (lane < past), 0.0, work[past:, :])
            work[past:, :] = old - update


def vmem_call(kernel, place, operands, out_shape, scratch_shapes, flops, name):
    smem, vmem = (pl.BlockSpec(memory_space=space) for space in (pltpu.SMEM, pltpu.VMEM))
    return pl.pallas_call(
        kernel,
        out_shape=out_shape,
        in_specs=[smem] + [vmem] * len(operands),
        out_specs=jax.tree.map(lambda _: vmem, out_shape),
        scratch_shapes=scratch_shapes,
        compiler_params=pltpu.CompilerParams(vmem_limit_bytes=12 * 2**20),
        cost_estimate=pl.CostEstimate(flops=flops, bytes_accessed=4 * 2**20, transcendentals=0),
        name=name,
    )(place, *operands)


def parts_kernel(place, mine, one, two, three, *outs):
    part = outs[0].shape[0]
    for steps, out in enumerate(outs):
        here = pl.ds(pl.multiple_of(((place[2] + steps) % SIDE) * part, part), part)
        out[...] = (mine[here, :] + two[here, :]) + (one[here, :] + three[here, :])


def finish_kernel(scale, place, inverse, mine, other, projected, turned):
    columns, wide = mine.shape
    part = columns // SIDE
    core = place[4]
    for source, side in ((mine, core), (other, 1 - core)):
        for steps in range(SIDE):
            here = pl.ds(pl.multiple_of(((place[2] + SIDE - steps) % SIDE) * part, part), part)
            turned[here, :] = source[pl.ds(steps * part, part), :]
        rows = lax.dot_general(turned[...].T, inverse[...], NT, precision=HIGH, preferred_element_type=F32)
        projected[pl.ds(pl.multiple_of(side * wide, wide), wide), :] = rows * scale


def on_device(activations, sketch_matrix, row_counts):
    rows_here, width = activations.shape
    columns = sketch_matrix.shape[1]
    square = jax.ShapeDtypeStruct((columns, columns), F32)
    total_rows = rows_here * lax.axis_size(BOTH)
    row, inner = lax.axis_index("rows"), lax.axis_index("inner")
    place = jnp.stack([row // SIDE, row % SIDE, inner // 2, inner, inner % 2]).astype(jnp.int32)

    held, sketch, split, gram_mine, gram_other = sketch_call(place, row_counts, activations, sketch_matrix)

    packed = gram_mine + swap_cores(gram_other)
    near_a = swap_cores(projection_call(place, split, held, (1, 3), 1))
    packed = pair_axis(packed, ("z", "x"))
    near_b = swap_cores(projection_call(place, split, held, (2, 0), 1))
    to_one, to_three = projection_call(place, split, held, (1, 3), 0, near_a)
    one = send(to_one, ("x", "y"), 1)
    three = send(to_three, ("x", "y"), 3)
    to_two, mine = projection_call(place, split, held, (2, 0), 0, near_b)
    two = send(to_two, ("x", "y"), 2)
    packed = pair_axis(packed, ("x", "y"))
    packed = pair_axis(packed, ("y", "z"))
    inverse = vmem_call(
        inverse_kernel, place, (packed, swap_cores(packed)), square, [pltpu.VMEM(square.shape, F32)],
        12 * columns**3, "inverse",
    )

    blocks = [(mine[j] + two[j]) + (one[j] + three[j]) for j in range(SIDE)]
    arrived = [send(blocks[j], ("y", "x"), j) for j in range(1, SIDE)]
    part = jax.ShapeDtypeStruct((columns // SIDE, WIDE), F32)
    parts = vmem_call(parts_kernel, place, (blocks[0], *arrived), [part] * SIDE, [], columns * WIDE, "parts")
    arrived = [send(parts[s], ("z", "z"), s) for s in range(1, SIDE)]
    total = (parts[0] + arrived[1]) + (arrived[0] + arrived[2])
    turned = jnp.concatenate([total] + [send(total, ("z", "z"), s) for s in range(1, SIDE)], 0)
    projected = vmem_call(
        lambda *refs: finish_kernel(math.sqrt(width / total_rows), *refs), place,
        (inverse, turned, swap_cores(turned)), jax.ShapeDtypeStruct((2 * WIDE, columns), F32),
        [pltpu.VMEM((columns, WIDE), F32)], 24 * columns**2 * WIDE, "finish",
    )
    basis = lax.dot_general(sketch, inverse, NT, precision=HIGH) * math.sqrt(total_rows)
    return (basis, projected)


def solution(mesh):
    return jax.shard_map(
        on_device,
        mesh=mesh,
        in_specs=(P(("rows", "inner"), None), P(), P(("rows", "inner"))),
        out_specs=(P(("rows", "inner"), None), P("rows", None)),
        check_vma=False,
    )
```

```python
import math

import jax
import jax.numpy as jnp
from jax import lax
from jax.experimental import pallas as pl
from jax.experimental.pallas import tpu as pltpu
from jax.sharding import PartitionSpec as P

SIDE = 4
BOTH = ("rows", "inner")
F32 = jnp.float32
BF16 = jnp.bfloat16
HIGH = lax.Precision.HIGHEST
NT = (((1,), (1,)), ((), ()))
TN = (((0,), (0,)), ((), ()))
GROUP = 8
PANEL = 64
AHEAD = 3
DEPTHS = (256, 512) + 9 * (768,) + (512,)
WIDE = 256


def device(y, x, z, core):
    return ((y % SIDE) * SIDE + x % SIDE) * 2 * SIDE + (z % SIDE) * 2 + core


def pairs(move):
    found = []
    for y in range(SIDE):
        for x in range(SIDE):
            for z in range(SIDE):
                for core in range(2):
                    found.append((device(y, x, z, core), device(*move(y, x, z, core))))
    return found


def step_on(axis, steps, y, x, z, core):
    return (y + steps * (axis == "y"), x + steps * (axis == "x"), z + steps * (axis == "z"), core)


def send(value, axes, steps):
    return lax.ppermute(value, BOTH, pairs(lambda y, x, z, core: step_on(axes[core], steps, y, x, z, core)))


def swap_cores(value):
    return lax.ppermute(value, BOTH, pairs(lambda y, x, z, core: (y, x, z, 1 - core)))


def add_partner(value, axes, partner):
    def move(y, x, z, core):
        at = {"y": y, "x": x, "z": z}
        at[axes[core]] = partner(at[axes[core]])
        return (at["y"], at["x"], at["z"], core)

    return value + lax.ppermute(value, BOTH, pairs(move))


def flip(i):
    return i ^ 1


def mirror(i):
    return SIDE - 1 - i


def sketch_kernel(place, count, act, test, held, sketch, split, gram_mine, gram_other, tests, act_sems, test_sems):
    rows, width = held.shape
    columns = sketch.shape[1]
    half = columns // 2
    copies, parts, first = [], [], 0
    for step, size in enumerate(DEPTHS):
        part = pl.ds(first, size)
        first += size
        parts.append(part)
        copies.append(
            (
                pltpu.make_async_copy(test.at[part, :], tests.at[part, :], test_sems.at[step]),
                pltpu.make_async_copy(act.at[:, part], held.at[:, part], act_sems.at[step]),
            )
        )
    for pair in copies[:AHEAD]:
        for copy in pair:
            copy.start()
    for step, (part, pair) in enumerate(zip(parts, copies)):
        for copy in pair:
            copy.wait()
        for copy in copies[step + AHEAD] if step + AHEAD < len(copies) else ():
            copy.start()
        product = jnp.dot(held[:, part], tests[part, :], preferred_element_type=F32)
        if step == 0:
            sketch[...] = product
        else:
            sketch[...] += product
    gram = jnp.zeros((columns, columns), F32)
    for first in range(0, rows, 256):
        here = pl.ds(first, 256)
        slots = lax.broadcasted_iota(jnp.int32, (256, columns), 0) + first
        live = jnp.where(slots < count[0], sketch[here, :], 0.0)
        sketch[here, :] = live
        turned = live.T
        high = turned.astype(BF16)
        split[:columns, here] = high
        split[columns:, here] = (turned - high.astype(F32)).astype(BF16)
        gram += lax.dot_general(turned, turned, NT, precision=HIGH, preferred_element_type=F32)
    core = place[4]
    upper = jnp.concatenate([gram[:half, :half], gram[: half // 2, half:]], 0)
    lower = jnp.concatenate([gram[half:, half:], gram[half // 2 : half, half:]], 0)
    gram_mine[...] = jnp.where(core == 0, upper, lower)
    gram_other[...] = jnp.where(core == 0, lower, upper)


def sketch_call(place, count, activations, sketch_matrix):
    rows, width = activations.shape
    columns = sketch_matrix.shape[1]
    packed = (columns // 2 + columns // 4, columns // 2)
    steps = len(DEPTHS)
    smem, anywhere, vmem = (pl.BlockSpec(memory_space=space) for space in (pltpu.SMEM, pltpu.HBM, pltpu.VMEM))
    return pl.pallas_call(
        sketch_kernel,
        out_shape=[
            pltpu.VMEM((rows, width), BF16),
            pltpu.VMEM((rows, columns), F32),
            pltpu.VMEM((2 * columns, rows), BF16),
            pltpu.VMEM(packed, F32),
            pltpu.VMEM(packed, F32),
        ],
        in_specs=[smem, smem, anywhere, anywhere],
        out_specs=[vmem] * 5,
        scratch_shapes=[
            pltpu.VMEM((width, columns), BF16),
            pltpu.SemaphoreType.DMA((steps,)),
            pltpu.SemaphoreType.DMA((steps,)),
        ],
        compiler_params=pltpu.CompilerParams(vmem_limit_bytes=12 * 2**20),
        cost_estimate=pl.CostEstimate(
            flops=2 * rows * width * columns, bytes_accessed=2 * width * (rows + columns), transcendentals=0
        ),
        name="sketch",
    )(place, count, *(pltpu.with_memory_space_constraint(value, pltpu.HBM) for value in (activations, sketch_matrix)))


def projection_kernel(offsets, other, place, split, held, after, *refs):
    columns = split.shape[0] // 2
    core = place[4] + other
    core = jnp.where(core == 2, 0, core)
    for i, (one, two) in enumerate(offsets):
        y = (place[0] + jnp.where(core == 0, two, one)) % SIDE
        x = (place[1] + jnp.where(core == 0, one, two)) % SIDE
        first = pl.multiple_of(((y * SIDE + x) * 2 + core) * WIDE, WIDE)
        both = jnp.dot(split[...], held[:, pl.ds(first, WIDE)], preferred_element_type=F32)
        block = both[:columns] + both[columns:]
        if other:
            refs[0][i] = block
        else:
            block = block + refs[0][i]
            refs[1 + i // SIDE][i % SIDE] = block


def projection_call(place, split, held, after, offsets, other, received=None):
    rows = held.shape[0]
    columns = split.shape[0] // 2
    smem, vmem = (pl.BlockSpec(memory_space=space) for space in (pltpu.SMEM, pltpu.VMEM))
    in_specs = [smem, vmem, vmem, pl.BlockSpec(memory_space=pl.ANY)]
    operands = [place, split, held, after]
    blocks = len(offsets)
    if other:
        out_shape = pltpu.VMEM((blocks, columns, WIDE), F32)
        out_specs = vmem
    else:
        in_specs.append(vmem)
        operands.append(received)
        out_shape = [pltpu.VMEM((SIDE, columns, WIDE), F32)] * (blocks // SIDE)
        out_specs = [vmem] * (blocks // SIDE)
    return pl.pallas_call(
        lambda *refs: projection_kernel(offsets, other, *refs),
        out_shape=out_shape,
        in_specs=in_specs,
        out_specs=out_specs,
        compiler_params=pltpu.CompilerParams(vmem_limit_bytes=8 * 2**20),
        cost_estimate=pl.CostEstimate(
            flops=4 * blocks * rows * WIDE * columns,
            bytes_accessed=blocks * 8 * WIDE * columns,
            transcendentals=0,
        ),
        name="projection",
    )(*operands)


def small_inverse(matrix):
    size = matrix.shape[0]
    groups = [matrix[first : first + GROUP, :] for first in range(0, size, GROUP)]
    lane = lax.broadcasted_iota(jnp.int32, (1, size), 1)
    sublane = lax.broadcasted_iota(jnp.int32, (GROUP, size), 0)
    for at in range(len(groups)):
        first = GROUP * at
        inside = (lane >= first) & (lane < first + GROUP)
        columns = [
            [jnp.broadcast_to(group[:, first + j : first + j + 1], (GROUP, size)) for j in range(GROUP)]
            for group in groups[at:]
        ]
        top = columns[0]
        scaled, done = [], []
        for j in range(GROUP):
            pivot = top[j][j : j + 1, :]
            reciprocal = 1.0 / pivot
            factors = [top[k][j : j + 1, :] * reciprocal for k in range(j + 1, GROUP)]
            for column in columns:
                for k, factor in enumerate(factors, j + 1):
                    column[k] = column[k] - column[j] * factor
            row = jnp.where(inside, 0.0, groups[at][j : j + 1, :])
            for i in range(j):
                row = row - top[i][j : j + 1, :] * scaled[i]
            row = jnp.where(lane == first + j, 1.0, row)
            scaled.append(row * reciprocal)
            done.append(row * lax.rsqrt(pivot))
        for below, column in enumerate(columns[1:], at + 1):
            rest = jnp.where(inside, 0.0, groups[below])
            for j in range(GROUP):
                rest = rest - column[j] * scaled[j]
            groups[below] = rest
        for j in range(GROUP):
            groups[at] = jnp.where(sublane == j, done[j], groups[at])
    rows, cols = (lax.broadcasted_iota(jnp.int32, (size, size), axis) for axis in (0, 1))
    return jnp.where(rows >= cols, jnp.concatenate(groups, 0), 0.0)


def inverse_kernel(place, mine, other, inverse, work):
    size = work.shape[0]
    half = size // 2
    core = place[4]
    upper = jnp.where(core == 0, mine[...], other[...])
    lower = jnp.where(core == 0, other[...], mine[...])
    corner = jnp.concatenate([upper[half:], lower[half:]], 0)
    work[:half, :half] = upper[:half]
    work[:half, half:] = corner
    work[half:, :half] = corner.T
    work[half:, half:] = lower[:half]
    for first in range(0, size, PANEL):
        past = first + PANEL
        rows = pl.ds(first, PANEL)
        block = small_inverse(work[rows, first:past])
        lane = lax.broadcasted_iota(jnp.int32, (PANEL, size), 1)
        parts = [jnp.zeros((PANEL, first), F32)] * (first > 0) + [block]
        parts += [jnp.zeros((PANEL, size - past), F32)] * (past < size)
        placed = jnp.concatenate(parts, 1) if len(parts) > 1 else block
        panel = jnp.dot(block, work[rows, :], precision=HIGH, preferred_element_type=F32)
        panel = jnp.where((lane >= first) & (lane < past), placed, panel)
        inverse[rows, :] = jnp.where(lane < past, panel, 0.0)
        if past < size:
            update = lax.dot_general(panel[:, past:], panel, TN, precision=HIGH, preferred_element_type=F32)
            lane = lax.broadcasted_iota(jnp.int32, (size - past, size), 1)
            old = jnp.where((lane >= first) & (lane < past), 0.0, work[past:, :])
            work[past:, :] = old - update


def vmem_call(kernel, place, operands, out_shape, scratch_shapes, flops, name):
    smem, vmem = (pl.BlockSpec(memory_space=space) for space in (pltpu.SMEM, pltpu.VMEM))
    return pl.pallas_call(
        kernel,
        out_shape=out_shape,
        in_specs=[smem] + [vmem] * len(operands),
        out_specs=jax.tree.map(lambda _: vmem, out_shape),
        scratch_shapes=scratch_shapes,
        compiler_params=pltpu.CompilerParams(vmem_limit_bytes=12 * 2**20),
        cost_estimate=pl.CostEstimate(flops=flops, bytes_accessed=4 * 2**20, transcendentals=0),
        name=name,
    )(place, *operands)


def parts_kernel(place, mine, one, two, three, *outs):
    part = outs[0].shape[0]
    for steps, out in enumerate(outs):
        here = pl.ds(pl.multiple_of(((place[2] + steps) % SIDE) * part, part), part)
        out[...] = (mine[here, :] + two[here, :]) + (one[here, :] + three[here, :])


def finish_kernel(scale, place, inverse, mine, other, projected, turned):
    columns, wide = mine.shape
    part = columns // SIDE
    core = place[4]
    for source, side in ((mine, core), (other, 1 - core)):
        for steps in range(SIDE):
            here = pl.ds(pl.multiple_of(((place[2] + SIDE - steps) % SIDE) * part, part), part)
            turned[here, :] = source[pl.ds(steps * part, part), :]
        rows = lax.dot_general(turned[...].T, inverse[...], NT, precision=HIGH, preferred_element_type=F32)
        projected[pl.ds(pl.multiple_of(side * wide, wide), wide), :] = rows * scale


def on_device(activations, sketch_matrix, row_counts):
    rows_here, width = activations.shape
    columns = sketch_matrix.shape[1]
    square = jax.ShapeDtypeStruct((columns, columns), F32)
    total_rows = rows_here * lax.axis_size(BOTH)
    row, inner = lax.axis_index("rows"), lax.axis_index("inner")
    place = jnp.stack([row // SIDE, row % SIDE, inner // 2, inner, inner % 2]).astype(jnp.int32)

    held, sketch, split, gram_mine, gram_other = sketch_call(place, row_counts, activations, sketch_matrix)

    first = [(one, two) for one in (1, 3) for two in range(SIDE)]
    second = [(one, two) for one in (2, 0) for two in range(SIDE)]
    first_far = swap_cores(projection_call(place, split, held, place, first, 1))
    packed = gram_mine + swap_cores(gram_other)
    second_far = swap_cores(projection_call(place, split, held, packed, second, 1))
    packed = add_partner(packed, ("z", "x"), flip)
    to_one, to_three = projection_call(place, split, held, packed, first, 0, first_far)
    one, three = send(to_one, ("x", "y"), 1), send(to_three, ("x", "y"), 3)
    packed = add_partner(packed, ("z", "x"), mirror)
    to_two, mine = projection_call(place, split, held, packed, second, 0, second_far)
    two = send(to_two, ("x", "y"), 2)
    for axes in (("x", "y"), ("y", "z")):
        for partner in (flip, mirror):
            packed = add_partner(packed, axes, partner)
    inverse = vmem_call(
        inverse_kernel, place, (packed, swap_cores(packed)), square, [pltpu.VMEM(square.shape, F32)],
        12 * columns**3, "inverse",
    )

    one, two, three, inverse = lax.optimization_barrier((one, two, three, inverse))
    blocks = [(mine[j] + two[j]) + (one[j] + three[j]) for j in range(SIDE)]
    arrived = [send(blocks[j], ("y", "x"), j) for j in range(1, SIDE)]
    part = jax.ShapeDtypeStruct((columns // SIDE, WIDE), F32)
    parts = vmem_call(parts_kernel, place, (blocks[0], *arrived), [part] * SIDE, [], columns * WIDE, "parts")
    arrived = [send(parts[s], ("z", "z"), s) for s in range(1, SIDE)]
    total = (parts[0] + arrived[1]) + (arrived[0] + arrived[2])
    turned = jnp.concatenate([total] + [send(total, ("z", "z"), s) for s in range(1, SIDE)], 0)
    projected = vmem_call(
        lambda *refs: finish_kernel(math.sqrt(width / total_rows), *refs), place,
        (inverse, turned, swap_cores(turned)), jax.ShapeDtypeStruct((2 * WIDE, columns), F32),
        [pltpu.VMEM((columns, WIDE), F32)], 24 * columns**2 * WIDE, "finish",
    )
    basis = lax.dot_general(sketch, inverse, NT, precision=HIGH) * math.sqrt(total_rows)
    return (basis, projected)


def solution(mesh):
    return jax.shard_map(
        on_device,
        mesh=mesh,
        in_specs=(P(("rows", "inner"), None), P(), P(("rows", "inner"))),
        out_specs=(P(("rows", "inner"), None), P("rows", None)),
        check_vma=False,
    )
```

```python
import math

import jax
import jax.numpy as jnp
from jax import lax
from jax.experimental import pallas as pl
from jax.experimental.pallas import tpu as pltpu
from jax.sharding import PartitionSpec as P

SIDE = 4
BOTH = ("rows", "inner")
F32 = jnp.float32
BF16 = jnp.bfloat16
HIGH = lax.Precision.HIGHEST
NT = (((1,), (1,)), ((), ()))
TN = (((0,), (0,)), ((), ()))
GROUP = 8
PANEL = 64
AHEAD = 3
DEPTHS = (512, 1024, 1536, 1536, 1536, 1024, 512, 512)
CHUNK = 128
WIDE = 256


def device(y, x, z, core):
    return ((y % SIDE) * SIDE + x % SIDE) * 2 * SIDE + (z % SIDE) * 2 + core


def pairs(move):
    found = []
    for y in range(SIDE):
        for x in range(SIDE):
            for z in range(SIDE):
                for core in range(2):
                    found.append((device(y, x, z, core), device(*move(y, x, z, core))))
    return found


def step_on(axis, steps, y, x, z, core):
    return (y + steps * (axis == "y"), x + steps * (axis == "x"), z + steps * (axis == "z"), core)


def send(value, axes, steps):
    return lax.ppermute(value, BOTH, pairs(lambda y, x, z, core: step_on(axes[core], steps, y, x, z, core)))


def swap_cores(value):
    return lax.ppermute(value, BOTH, pairs(lambda y, x, z, core: (y, x, z, 1 - core)))


def add_partner(value, axes, partner, beside=None):
    def move(y, x, z, core):
        at = {"y": y, "x": x, "z": z}
        at[axes[core]] = partner(at[axes[core]])
        return (at["y"], at["x"], at["z"], core)

    arrived = lax.ppermute(value, BOTH, pairs(move))
    if beside is None:
        return value + arrived
    arrived, beside = lax.optimization_barrier((arrived, beside))
    return value + arrived, beside


def flip(i):
    return i ^ 1


def mirror(i):
    return SIDE - 1 - i


def sketch_kernel(place, count, act, test, held, sketch, split, gram_mine, gram_other, tests, act_sems, test_sems):
    rows, width = held.shape
    columns = sketch.shape[1]
    half = columns // 2
    copies, parts, first = [], [], 0
    for step, size in enumerate(DEPTHS):
        part = pl.ds(first, size)
        first += size
        parts.append(part)
        copies.append(
            (
                pltpu.make_async_copy(test.at[part, :], tests.at[part, :], test_sems.at[step]),
                pltpu.make_async_copy(act.at[:, part], held.at[:, part], act_sems.at[step]),
            )
        )
    for pair in copies[:AHEAD]:
        for copy in pair:
            copy.start()
    for step, (part, pair) in enumerate(zip(parts, copies)):
        for copy in pair:
            copy.wait()
        for copy in copies[step + AHEAD] if step + AHEAD < len(copies) else ():
            copy.start()
        for first in range(0, rows, CHUNK):
            here = pl.ds(first, CHUNK)
            product = jnp.dot(held[here, part], tests[part, :], preferred_element_type=F32)
            if step == 0:
                sketch[here, :] = product
            else:
                sketch[here, :] += product
    gram = jnp.zeros((columns, columns), F32)
    for first in range(0, rows, 256):
        here = pl.ds(first, 256)
        slots = lax.broadcasted_iota(jnp.int32, (256, columns), 0) + first
        live = jnp.where(slots < count[0], sketch[here, :], 0.0)
        sketch[here, :] = live
        turned = live.T
        high = turned.astype(BF16)
        split[:columns, here] = high
        split[columns:, here] = (turned - high.astype(F32)).astype(BF16)
        gram += lax.dot_general(turned, turned, NT, precision=HIGH, preferred_element_type=F32)
    core = place[4]
    upper = jnp.concatenate([gram[:half, :half], gram[: half // 2, half:]], 0)
    lower = jnp.concatenate([gram[half:, half:], gram[half // 2 : half, half:]], 0)
    gram_mine[...] = jnp.where(core == 0, upper, lower)
    gram_other[...] = jnp.where(core == 0, lower, upper)


def sketch_call(place, count, activations, sketch_matrix):
    rows, width = activations.shape
    columns = sketch_matrix.shape[1]
    packed = (columns // 2 + columns // 4, columns // 2)
    steps = len(DEPTHS)
    smem, anywhere, vmem = (pl.BlockSpec(memory_space=space) for space in (pltpu.SMEM, pltpu.HBM, pltpu.VMEM))
    return pl.pallas_call(
        sketch_kernel,
        out_shape=[
            pltpu.VMEM((rows, width), BF16),
            pltpu.VMEM((rows, columns), F32),
            pltpu.VMEM((2 * columns, rows), BF16),
            pltpu.VMEM(packed, F32),
            pltpu.VMEM(packed, F32),
        ],
        in_specs=[smem, smem, anywhere, anywhere],
        out_specs=[vmem] * 5,
        scratch_shapes=[
            pltpu.VMEM((width, columns), BF16),
            pltpu.SemaphoreType.DMA((steps,)),
            pltpu.SemaphoreType.DMA((steps,)),
        ],
        compiler_params=pltpu.CompilerParams(vmem_limit_bytes=12 * 2**20),
        cost_estimate=pl.CostEstimate(
            flops=2 * rows * width * columns, bytes_accessed=2 * width * (rows + columns), transcendentals=0
        ),
        name="sketch",
    )(place, count, *(pltpu.with_memory_space_constraint(value, pltpu.HBM) for value in (activations, sketch_matrix)))


def projection_kernel(offsets, other, place, split, held, after, *refs):
    columns = split.shape[0] // 2
    core = place[4] + other
    core = jnp.where(core == 2, 0, core)
    for i, (one, two) in enumerate(offsets):
        y = (place[0] + jnp.where(core == 0, two, one)) % SIDE
        x = (place[1] + jnp.where(core == 0, one, two)) % SIDE
        first = pl.multiple_of(((y * SIDE + x) * 2 + core) * WIDE, WIDE)
        both = jnp.dot(split[...], held[:, pl.ds(first, WIDE)], preferred_element_type=F32)
        block = both[:columns] + both[columns:]
        if other:
            refs[0][i] = block
        else:
            block = block + refs[0][i]
            refs[1 + i // SIDE][i % SIDE] = block


def projection_call(place, split, held, after, offsets, other, received=None):
    rows = held.shape[0]
    columns = split.shape[0] // 2
    smem, vmem = (pl.BlockSpec(memory_space=space) for space in (pltpu.SMEM, pltpu.VMEM))
    in_specs = [smem, vmem, vmem, pl.BlockSpec(memory_space=pl.ANY)]
    operands = [place, split, held, after]
    blocks = len(offsets)
    if other:
        out_shape = pltpu.VMEM((blocks, columns, WIDE), F32)
        out_specs = vmem
    else:
        in_specs.append(vmem)
        operands.append(received)
        out_shape = [pltpu.VMEM((SIDE, columns, WIDE), F32)] * (blocks // SIDE)
        out_specs = [vmem] * (blocks // SIDE)
    return pl.pallas_call(
        lambda *refs: projection_kernel(offsets, other, *refs),
        out_shape=out_shape,
        in_specs=in_specs,
        out_specs=out_specs,
        compiler_params=pltpu.CompilerParams(vmem_limit_bytes=8 * 2**20),
        cost_estimate=pl.CostEstimate(
            flops=4 * blocks * rows * WIDE * columns,
            bytes_accessed=blocks * 8 * WIDE * columns,
            transcendentals=0,
        ),
        name="projection",
    )(*operands)


def small_inverse(matrix):
    size = matrix.shape[0]
    groups = [matrix[first : first + GROUP, :] for first in range(0, size, GROUP)]
    lane = lax.broadcasted_iota(jnp.int32, (1, size), 1)
    sublane = lax.broadcasted_iota(jnp.int32, (GROUP, size), 0)
    for at in range(len(groups)):
        first = GROUP * at
        inside = (lane >= first) & (lane < first + GROUP)
        columns = [
            [jnp.broadcast_to(group[:, first + j : first + j + 1], (GROUP, size)) for j in range(GROUP)]
            for group in groups[at:]
        ]
        top = columns[0]
        scaled, done = [], []
        for j in range(GROUP):
            pivot = top[j][j : j + 1, :]
            reciprocal = 1.0 / pivot
            factors = [top[k][j : j + 1, :] * reciprocal for k in range(j + 1, GROUP)]
            for column in columns:
                for k, factor in enumerate(factors, j + 1):
                    column[k] = column[k] - column[j] * factor
            row = jnp.where(inside, 0.0, groups[at][j : j + 1, :])
            for i in range(j):
                row = row - top[i][j : j + 1, :] * scaled[i]
            row = jnp.where(lane == first + j, 1.0, row)
            scaled.append(row * reciprocal)
            done.append(row * lax.rsqrt(pivot))
        for below, column in enumerate(columns[1:], at + 1):
            rest = jnp.where(inside, 0.0, groups[below])
            for j in range(GROUP):
                rest = rest - column[j] * scaled[j]
            groups[below] = rest
        for j in range(GROUP):
            groups[at] = jnp.where(sublane == j, done[j], groups[at])
    rows, cols = (lax.broadcasted_iota(jnp.int32, (size, size), axis) for axis in (0, 1))
    return jnp.where(rows >= cols, jnp.concatenate(groups, 0), 0.0)


def inverse_kernel(place, mine, other, inverse, work):
    size = work.shape[0]
    half = size // 2
    core = place[4]
    upper = jnp.where(core == 0, mine[...], other[...])
    lower = jnp.where(core == 0, other[...], mine[...])
    corner = jnp.concatenate([upper[half:], lower[half:]], 0)
    work[:half, :half] = upper[:half]
    work[:half, half:] = corner
    work[half:, :half] = corner.T
    work[half:, half:] = lower[:half]
    for first in range(0, size, PANEL):
        past = first + PANEL
        rows = pl.ds(first, PANEL)
        block = small_inverse(work[rows, first:past])
        lane = lax.broadcasted_iota(jnp.int32, (PANEL, size), 1)
        parts = [jnp.zeros((PANEL, first), F32)] * (first > 0) + [block]
        parts += [jnp.zeros((PANEL, size - past), F32)] * (past < size)
        placed = jnp.concatenate(parts, 1) if len(parts) > 1 else block
        panel = jnp.dot(block, work[rows, :], precision=HIGH, preferred_element_type=F32)
        panel = jnp.where((lane >= first) & (lane < past), placed, panel)
        inverse[rows, :] = jnp.where(lane < past, panel, 0.0)
        if past < size:
            update = lax.dot_general(panel[:, past:], panel, TN, precision=HIGH, preferred_element_type=F32)
            lane = lax.broadcasted_iota(jnp.int32, (size - past, size), 1)
            old = jnp.where((lane >= first) & (lane < past), 0.0, work[past:, :])
            work[past:, :] = old - update


def vmem_call(kernel, place, operands, out_shape, scratch_shapes, flops, name):
    smem, vmem = (pl.BlockSpec(memory_space=space) for space in (pltpu.SMEM, pltpu.VMEM))
    return pl.pallas_call(
        kernel,
        out_shape=out_shape,
        in_specs=[smem] + [vmem] * len(operands),
        out_specs=jax.tree.map(lambda _: vmem, out_shape),
        scratch_shapes=scratch_shapes,
        compiler_params=pltpu.CompilerParams(vmem_limit_bytes=12 * 2**20),
        cost_estimate=pl.CostEstimate(flops=flops, bytes_accessed=4 * 2**20, transcendentals=0),
        name=name,
    )(place, *operands)


def parts_kernel(place, mine, one, two, three, *outs):
    part = outs[0].shape[0]
    for steps, out in enumerate(outs):
        here = pl.ds(pl.multiple_of(((place[2] + steps) % SIDE) * part, part), part)
        out[...] = (mine[here, :] + two[here, :]) + (one[here, :] + three[here, :])


def finish_kernel(scale, place, inverse, mine, other, projected, turned):
    columns, wide = mine.shape
    part = columns // SIDE
    core = place[4]
    for source, side in ((mine, core), (other, 1 - core)):
        for steps in range(SIDE):
            here = pl.ds(pl.multiple_of(((place[2] + SIDE - steps) % SIDE) * part, part), part)
            turned[here, :] = source[pl.ds(steps * part, part), :]
        rows = lax.dot_general(turned[...].T, inverse[...], NT, precision=HIGH, preferred_element_type=F32)
        projected[pl.ds(pl.multiple_of(side * wide, wide), wide), :] = rows * scale


def on_device(activations, sketch_matrix, row_counts):
    rows_here, width = activations.shape
    columns = sketch_matrix.shape[1]
    square = jax.ShapeDtypeStruct((columns, columns), F32)
    total_rows = rows_here * lax.axis_size(BOTH)
    row, inner = lax.axis_index("rows"), lax.axis_index("inner")
    place = jnp.stack([row // SIDE, row % SIDE, inner // 2, inner, inner % 2]).astype(jnp.int32)

    held, sketch, split, gram_mine, gram_other = sketch_call(place, row_counts, activations, sketch_matrix)

    first = [(one, two) for one in (1, 3) for two in range(SIDE)]
    second = [(one, two) for one in (2, 0) for two in range(SIDE)]
    first_far = swap_cores(projection_call(place, split, held, place, first, 1))
    packed = gram_mine + swap_cores(gram_other)
    second_far = projection_call(place, split, held, packed, second, 1)
    packed, second_far = add_partner(packed, ("x", "y"), flip, second_far)
    second_far = swap_cores(second_far)
    near = projection_call(place, split, held, packed, first, 0, first_far)
    packed, (to_one, to_three) = add_partner(packed, ("x", "y"), mirror, near)
    near = projection_call(place, split, held, packed, second, 0, second_far)
    packed, (to_two, mine) = add_partner(packed, ("y", "x"), flip, near)
    packed = add_partner(packed, ("y", "x"), mirror)
    to_one, to_three, to_two, packed = lax.optimization_barrier((to_one, to_three, to_two, packed))
    one, three = send(to_one, ("x", "y"), 1), send(to_three, ("x", "y"), 3)
    two = send(to_two, ("x", "y"), 2)
    packed = add_partner(packed, ("z", "z"), flip)
    packed = add_partner(packed, ("z", "z"), mirror)
    inverse = vmem_call(
        inverse_kernel, place, (packed, swap_cores(packed)), square, [pltpu.VMEM(square.shape, F32)],
        12 * columns**3, "inverse",
    )
    basis = lax.dot_general(sketch, inverse, NT, precision=HIGH) * math.sqrt(total_rows)

    one, two, three, inverse, basis = lax.optimization_barrier((one, two, three, inverse, basis))
    blocks = [(mine[j] + two[j]) + (one[j] + three[j]) for j in range(SIDE)]
    arrived = [send(blocks[j], ("y", "x"), j) for j in range(1, SIDE)]
    part = jax.ShapeDtypeStruct((columns // SIDE, WIDE), F32)
    parts = vmem_call(parts_kernel, place, (blocks[0], *arrived), [part] * SIDE, [], columns * WIDE, "parts")
    arrived = [send(parts[s], ("z", "z"), s) for s in range(1, SIDE)]
    total = (parts[0] + arrived[1]) + (arrived[0] + arrived[2])
    turned = jnp.concatenate([total] + [send(total, ("z", "z"), s) for s in range(1, SIDE)], 0)
    projected = vmem_call(
        lambda *refs: finish_kernel(math.sqrt(width / total_rows), *refs), place,
        (inverse, turned, swap_cores(turned)), jax.ShapeDtypeStruct((2 * WIDE, columns), F32),
        [pltpu.VMEM((columns, WIDE), F32)], 24 * columns**2 * WIDE, "finish",
    )
    return (basis, projected)


def solution(mesh):
    return jax.shard_map(
        on_device,
        mesh=mesh,
        in_specs=(P(("rows", "inner"), None), P(), P(("rows", "inner"))),
        out_specs=(P(("rows", "inner"), None), P("rows", None)),
        check_vma=False,
    )
```

```python
import math

import jax
import jax.numpy as jnp
from jax import lax
from jax.experimental import pallas as pl
from jax.experimental.pallas import tpu as pltpu
from jax.sharding import PartitionSpec as P

SIDE = 4
BOTH = ("rows", "inner")
F32 = jnp.float32
BF16 = jnp.bfloat16
HIGH = lax.Precision.HIGHEST
NT = (((1,), (1,)), ((), ()))
TN = (((0,), (0,)), ((), ()))
GROUP = 8
PANEL = 64
AHEAD = 3
DEPTHS = (512, 1024, 1536, 1536, 1536, 1024, 512, 512)
CHUNK = 128
WIDE = 256


def device(y, x, z, core):
    return ((y % SIDE) * SIDE + x % SIDE) * 2 * SIDE + (z % SIDE) * 2 + core


def pairs(move):
    found = []
    for y in range(SIDE):
        for x in range(SIDE):
            for z in range(SIDE):
                for core in range(2):
                    found.append((device(y, x, z, core), device(*move(y, x, z, core))))
    return found


def step_on(axis, steps, y, x, z, core):
    return (y + steps * (axis == "y"), x + steps * (axis == "x"), z + steps * (axis == "z"), core)


def send(value, axes, steps):
    return lax.ppermute(value, BOTH, pairs(lambda y, x, z, core: step_on(axes[core], steps, y, x, z, core)))


def swap_cores(value):
    return lax.ppermute(value, BOTH, pairs(lambda y, x, z, core: (y, x, z, 1 - core)))


def add_partner(value, axes, partner, beside=None):
    def move(y, x, z, core):
        at = {"y": y, "x": x, "z": z}
        at[axes[core]] = partner(at[axes[core]])
        return (at["y"], at["x"], at["z"], core)

    arrived = lax.ppermute(value, BOTH, pairs(move))
    if beside is None:
        return value + arrived
    arrived, beside = lax.optimization_barrier((arrived, beside))
    return value + arrived, beside


def flip(i):
    return i ^ 1


def mirror(i):
    return SIDE - 1 - i


def sketch_kernel(place, count, act, test, held, sketch, split, gram_mine, gram_other, tests, act_sems, test_sems):
    rows, width = held.shape
    columns = sketch.shape[1]
    half = columns // 2
    copies, parts, first = [], [], 0
    for step, size in enumerate(DEPTHS):
        part = pl.ds(first, size)
        first += size
        parts.append(part)
        copies.append(
            (
                pltpu.make_async_copy(test.at[part, :], tests.at[part, :], test_sems.at[step]),
                pltpu.make_async_copy(act.at[:, part], held.at[:, part], act_sems.at[step]),
            )
        )
    for pair in copies[:AHEAD]:
        for copy in pair:
            copy.start()
    for step, (part, pair) in enumerate(zip(parts, copies)):
        for copy in pair:
            copy.wait()
        for copy in copies[step + AHEAD] if step + AHEAD < len(copies) else ():
            copy.start()
        for first in range(0, rows, CHUNK):
            here = pl.ds(first, CHUNK)
            product = jnp.dot(held[here, part], tests[part, :], preferred_element_type=F32)
            if step == 0:
                sketch[here, :] = product
            else:
                sketch[here, :] += product
    gram = jnp.zeros((columns, columns), F32)
    for first in range(0, rows, 256):
        here = pl.ds(first, 256)
        slots = lax.broadcasted_iota(jnp.int32, (256, columns), 0) + first
        live = jnp.where(slots < count[0], sketch[here, :], 0.0)
        sketch[here, :] = live
        turned = live.T
        high = turned.astype(BF16)
        split[:columns, here] = high
        split[columns:, here] = (turned - high.astype(F32)).astype(BF16)
        gram += lax.dot_general(turned, turned, NT, precision=HIGH, preferred_element_type=F32)
    core = place[4]
    upper = jnp.concatenate([gram[:half, :half], gram[: half // 2, half:]], 0)
    lower = jnp.concatenate([gram[half:, half:], gram[half // 2 : half, half:]], 0)
    gram_mine[...] = jnp.where(core == 0, upper, lower)
    gram_other[...] = jnp.where(core == 0, lower, upper)


def sketch_call(place, count, activations, sketch_matrix):
    rows, width = activations.shape
    columns = sketch_matrix.shape[1]
    packed = (columns // 2 + columns // 4, columns // 2)
    steps = len(DEPTHS)
    smem, anywhere, vmem = (pl.BlockSpec(memory_space=space) for space in (pltpu.SMEM, pltpu.HBM, pltpu.VMEM))
    return pl.pallas_call(
        sketch_kernel,
        out_shape=[
            pltpu.VMEM((rows, width), BF16),
            pltpu.VMEM((rows, columns), F32),
            pltpu.VMEM((2 * columns, rows), BF16),
            pltpu.VMEM(packed, F32),
            pltpu.VMEM(packed, F32),
        ],
        in_specs=[smem, smem, anywhere, anywhere],
        out_specs=[vmem] * 5,
        scratch_shapes=[
            pltpu.VMEM((width, columns), BF16),
            pltpu.SemaphoreType.DMA((steps,)),
            pltpu.SemaphoreType.DMA((steps,)),
        ],
        compiler_params=pltpu.CompilerParams(vmem_limit_bytes=12 * 2**20),
        cost_estimate=pl.CostEstimate(
            flops=2 * rows * width * columns, bytes_accessed=2 * width * (rows + columns), transcendentals=0
        ),
        name="sketch",
    )(place, count, *(pltpu.with_memory_space_constraint(value, pltpu.HBM) for value in (activations, sketch_matrix)))


def projection_kernel(offsets, other, place, split, held, after, *refs):
    columns = split.shape[0] // 2
    core = place[4] + other
    core = jnp.where(core == 2, 0, core)
    for i, (one, two) in enumerate(offsets):
        y = (place[0] + jnp.where(core == 0, two, one)) % SIDE
        x = (place[1] + jnp.where(core == 0, one, two)) % SIDE
        first = pl.multiple_of(((y * SIDE + x) * 2 + core) * WIDE, WIDE)
        both = jnp.dot(split[...], held[:, pl.ds(first, WIDE)], preferred_element_type=F32)
        block = both[:columns] + both[columns:]
        if other:
            refs[0][i] = block
        else:
            block = block + refs[0][i]
            refs[1 + i // SIDE][i % SIDE] = block


def projection_call(place, split, held, after, offsets, other, received=None):
    rows = held.shape[0]
    columns = split.shape[0] // 2
    smem, vmem = (pl.BlockSpec(memory_space=space) for space in (pltpu.SMEM, pltpu.VMEM))
    in_specs = [smem, vmem, vmem, pl.BlockSpec(memory_space=pl.ANY)]
    operands = [place, split, held, after]
    blocks = len(offsets)
    if other:
        out_shape = pltpu.VMEM((blocks, columns, WIDE), F32)
        out_specs = vmem
    else:
        in_specs.append(vmem)
        operands.append(received)
        out_shape = [pltpu.VMEM((SIDE, columns, WIDE), F32)] * (blocks // SIDE)
        out_specs = [vmem] * (blocks // SIDE)
    return pl.pallas_call(
        lambda *refs: projection_kernel(offsets, other, *refs),
        out_shape=out_shape,
        in_specs=in_specs,
        out_specs=out_specs,
        compiler_params=pltpu.CompilerParams(vmem_limit_bytes=8 * 2**20),
        cost_estimate=pl.CostEstimate(
            flops=4 * blocks * rows * WIDE * columns,
            bytes_accessed=blocks * 8 * WIDE * columns,
            transcendentals=0,
        ),
        name="projection",
    )(*operands)


def small_inverse(matrix):
    size = matrix.shape[0]
    groups = [matrix[first : first + GROUP, :] for first in range(0, size, GROUP)]
    lane = lax.broadcasted_iota(jnp.int32, (1, size), 1)
    sublane = lax.broadcasted_iota(jnp.int32, (GROUP, size), 0)
    for at in range(len(groups)):
        first = GROUP * at
        inside = (lane >= first) & (lane < first + GROUP)
        columns = [
            [jnp.broadcast_to(group[:, first + j : first + j + 1], (GROUP, size)) for j in range(GROUP)]
            for group in groups[at:]
        ]
        top = columns[0]
        scaled, done = [], []
        for j in range(GROUP):
            pivot = top[j][j : j + 1, :]
            reciprocal = 1.0 / pivot
            factors = [top[k][j : j + 1, :] * reciprocal for k in range(j + 1, GROUP)]
            for column in columns:
                for k, factor in enumerate(factors, j + 1):
                    column[k] = column[k] - column[j] * factor
            row = jnp.where(inside, 0.0, groups[at][j : j + 1, :])
            for i in range(j):
                row = row - top[i][j : j + 1, :] * scaled[i]
            row = jnp.where(lane == first + j, 1.0, row)
            scaled.append(row * reciprocal)
            done.append(row * lax.rsqrt(pivot))
        for below, column in enumerate(columns[1:], at + 1):
            rest = jnp.where(inside, 0.0, groups[below])
            for j in range(GROUP):
                rest = rest - column[j] * scaled[j]
            groups[below] = rest
        for j in range(GROUP):
            groups[at] = jnp.where(sublane == j, done[j], groups[at])
    rows, cols = (lax.broadcasted_iota(jnp.int32, (size, size), axis) for axis in (0, 1))
    return jnp.where(rows >= cols, jnp.concatenate(groups, 0), 0.0)


def inverse_kernel(place, mine, other, inverse, work):
    size = work.shape[0]
    half = size // 2
    core = place[4]
    upper = jnp.where(core == 0, mine[...], other[...])
    lower = jnp.where(core == 0, other[...], mine[...])
    corner = jnp.concatenate([upper[half:], lower[half:]], 0)
    work[:half, :half] = upper[:half]
    work[:half, half:] = corner
    work[half:, :half] = corner.T
    work[half:, half:] = lower[:half]
    for first in range(0, size, PANEL):
        past = first + PANEL
        rows = pl.ds(first, PANEL)
        block = small_inverse(work[rows, first:past])
        lane = lax.broadcasted_iota(jnp.int32, (PANEL, size), 1)
        parts = [jnp.zeros((PANEL, first), F32)] * (first > 0) + [block]
        parts += [jnp.zeros((PANEL, size - past), F32)] * (past < size)
        placed = jnp.concatenate(parts, 1) if len(parts) > 1 else block
        panel = jnp.dot(block, work[rows, :], precision=HIGH, preferred_element_type=F32)
        panel = jnp.where((lane >= first) & (lane < past), placed, panel)
        inverse[rows, :] = jnp.where(lane < past, panel, 0.0)
        if past < size:
            update = lax.dot_general(panel[:, past:], panel, TN, precision=HIGH, preferred_element_type=F32)
            lane = lax.broadcasted_iota(jnp.int32, (size - past, size), 1)
            old = jnp.where((lane >= first) & (lane < past), 0.0, work[past:, :])
            work[past:, :] = old - update


def vmem_call(kernel, place, operands, out_shape, scratch_shapes, flops, name):
    smem, vmem = (pl.BlockSpec(memory_space=space) for space in (pltpu.SMEM, pltpu.VMEM))
    return pl.pallas_call(
        kernel,
        out_shape=out_shape,
        in_specs=[smem] + [vmem] * len(operands),
        out_specs=jax.tree.map(lambda _: vmem, out_shape),
        scratch_shapes=scratch_shapes,
        compiler_params=pltpu.CompilerParams(vmem_limit_bytes=12 * 2**20),
        cost_estimate=pl.CostEstimate(flops=flops, bytes_accessed=4 * 2**20, transcendentals=0),
        name=name,
    )(place, *operands)


def parts_kernel(place, mine, one, two, three, *outs):
    part = outs[0].shape[0]
    for steps, out in enumerate(outs):
        here = pl.ds(pl.multiple_of(((place[2] + steps) % SIDE) * part, part), part)
        out[...] = (mine[here, :] + two[here, :]) + (one[here, :] + three[here, :])


def finish_kernel(scale, place, inverse, mine, other, projected, turned):
    columns, wide = mine.shape
    part = columns // SIDE
    core = place[4]
    for source, side in ((mine, core), (other, 1 - core)):
        for steps in range(SIDE):
            here = pl.ds(pl.multiple_of(((place[2] + SIDE - steps) % SIDE) * part, part), part)
            turned[here, :] = source[pl.ds(steps * part, part), :]
        rows = lax.dot_general(turned[...].T, inverse[...], NT, precision=HIGH, preferred_element_type=F32)
        projected[pl.ds(pl.multiple_of(side * wide, wide), wide), :] = rows * scale


def on_device(activations, sketch_matrix, row_counts):
    rows_here, width = activations.shape
    columns = sketch_matrix.shape[1]
    square = jax.ShapeDtypeStruct((columns, columns), F32)
    total_rows = rows_here * lax.axis_size(BOTH)
    row, inner = lax.axis_index("rows"), lax.axis_index("inner")
    place = jnp.stack([row // SIDE, row % SIDE, inner // 2, inner, inner % 2]).astype(jnp.int32)

    held, sketch, split, gram_mine, gram_other = sketch_call(place, row_counts, activations, sketch_matrix)

    first = [(one, two) for one in (1, 3) for two in range(SIDE)]
    second = [(one, two) for one in (2, 0) for two in range(SIDE)]
    first_far = swap_cores(projection_call(place, split, held, place, first, 1))
    packed = gram_mine + swap_cores(gram_other)
    second_far = projection_call(place, split, held, packed, second, 1)
    packed, second_far = add_partner(packed, ("x", "y"), flip, second_far)
    second_far = swap_cores(second_far)
    near = projection_call(place, split, held, packed, first, 0, first_far)
    packed, near = add_partner(packed, ("x", "y"), mirror, near)
    near, packed = lax.optimization_barrier((near, packed))
    one, three = send(near[0], ("x", "y"), 1), send(near[1], ("x", "y"), 3)
    near = projection_call(place, split, held, packed, second, 0, second_far)
    packed, (to_two, mine) = add_partner(packed, ("y", "x"), flip, near)
    two = send(to_two, ("x", "y"), 2)
    packed = add_partner(packed, ("z", "z"), flip)
    packed = add_partner(packed, ("z", "z"), mirror)
    packed = add_partner(packed, ("y", "x"), mirror)
    swapped = swap_cores(packed)

    one, two, three, packed = lax.optimization_barrier((one, two, three, packed))
    blocks = [(mine[j] + two[j]) + (one[j] + three[j]) for j in range(SIDE)]
    arrived = [send(blocks[j], ("y", "x"), j) for j in range(1, SIDE)]
    packed, swapped, blocks = lax.optimization_barrier((packed, swapped, blocks))
    inverse = vmem_call(
        inverse_kernel, place, (packed, swapped), square, [pltpu.VMEM(square.shape, F32)], 8 * 10**9, "inverse"
    )
    arrived, inverse = lax.optimization_barrier((arrived, inverse))
    part = jax.ShapeDtypeStruct((columns // SIDE, WIDE), F32)
    parts = vmem_call(parts_kernel, place, (blocks[0], *arrived), [part] * SIDE, [], columns * WIDE, "parts")
    arrived = [send(parts[s], ("z", "z"), s) for s in range(1, SIDE)]
    inverse, mine = lax.optimization_barrier((inverse, parts[0]))
    basis = lax.dot_general(sketch, inverse, NT, precision=HIGH) * math.sqrt(total_rows)
    arrived, basis = lax.optimization_barrier((arrived, basis))
    total = (parts[0] + arrived[1]) + (arrived[0] + arrived[2])
    turned = jnp.concatenate([total] + [send(total, ("z", "z"), s) for s in range(1, SIDE)], 0)
    projected = vmem_call(
        lambda *refs: finish_kernel(math.sqrt(width / total_rows), *refs), place,
        (inverse, turned, swap_cores(turned)), jax.ShapeDtypeStruct((2 * WIDE, columns), F32),
        [pltpu.VMEM((columns, WIDE), F32)], 24 * columns**2 * WIDE, "finish",
    )
    return (basis, projected)


def solution(mesh):
    return jax.shard_map(
        on_device,
        mesh=mesh,
        in_specs=(P(("rows", "inner"), None), P(), P(("rows", "inner"))),
        out_specs=(P(("rows", "inner"), None), P("rows", None)),
        check_vma=False,
    )
```

```python
import math

import jax
import jax.numpy as jnp
from jax import lax
from jax.experimental import pallas as pl
from jax.experimental.pallas import tpu as pltpu
from jax.sharding import PartitionSpec as P

SIDE = 4
BOTH = ("rows", "inner")
F32 = jnp.float32
BF16 = jnp.bfloat16
HIGH = lax.Precision.HIGHEST
NT = (((1,), (1,)), ((), ()))
TN = (((0,), (0,)), ((), ()))
GROUP = 8
PANEL = 64
AHEAD = 3
DEPTHS = (512, 1024, 1536, 1536, 1536, 1024, 512, 512)
CHUNK = 128
WIDE = 256


def device(y, x, z, core):
    return ((y % SIDE) * SIDE + x % SIDE) * 2 * SIDE + (z % SIDE) * 2 + core


def pairs(move):
    found = []
    for y in range(SIDE):
        for x in range(SIDE):
            for z in range(SIDE):
                for core in range(2):
                    found.append((device(y, x, z, core), device(*move(y, x, z, core))))
    return found


def step_on(axis, steps, y, x, z, core):
    return (y + steps * (axis == "y"), x + steps * (axis == "x"), z + steps * (axis == "z"), core)


def send(value, axes, steps):
    return lax.ppermute(value, BOTH, pairs(lambda y, x, z, core: step_on(axes[core], steps, y, x, z, core)))


def swap_cores(value):
    return lax.ppermute(value, BOTH, pairs(lambda y, x, z, core: (y, x, z, 1 - core)))


def add_partner(value, axes, partner, beside=None):
    def move(y, x, z, core):
        at = {"y": y, "x": x, "z": z}
        at[axes[core]] = partner(at[axes[core]])
        return (at["y"], at["x"], at["z"], core)

    arrived = lax.ppermute(value, BOTH, pairs(move))
    if beside is None:
        return value + arrived
    arrived, beside = lax.optimization_barrier((arrived, beside))
    return value + arrived, beside


def flip(i):
    return i ^ 1


def mirror(i):
    return SIDE - 1 - i


def sketch_kernel(place, count, act, test, held, sketch, split, gram_mine, gram_other, tests, act_sems, test_sems):
    rows, width = held.shape
    columns = sketch.shape[1]
    half = columns // 2
    copies, parts, first = [], [], 0
    for step, size in enumerate(DEPTHS):
        part = pl.ds(first, size)
        first += size
        parts.append(part)
        copies.append(
            (
                pltpu.make_async_copy(test.at[part, :], tests.at[part, :], test_sems.at[step]),
                pltpu.make_async_copy(act.at[:, part], held.at[:, part], act_sems.at[step]),
            )
        )
    for pair in copies[:AHEAD]:
        for copy in pair:
            copy.start()
    for step, (part, pair) in enumerate(zip(parts, copies)):
        for copy in pair:
            copy.wait()
        for copy in copies[step + AHEAD] if step + AHEAD < len(copies) else ():
            copy.start()
        for first in range(0, rows, CHUNK):
            here = pl.ds(first, CHUNK)
            product = jnp.dot(held[here, part], tests[part, :], preferred_element_type=F32)
            if step == 0:
                sketch[here, :] = product
            else:
                sketch[here, :] += product
    gram = jnp.zeros((columns, columns), F32)
    for first in range(0, rows, 256):
        here = pl.ds(first, 256)
        slots = lax.broadcasted_iota(jnp.int32, (256, columns), 0) + first
        live = jnp.where(slots < count[0], sketch[here, :], 0.0)
        sketch[here, :] = live
        turned = live.T
        high = turned.astype(BF16)
        split[:columns, here] = high
        split[columns:, here] = (turned - high.astype(F32)).astype(BF16)
        gram += lax.dot_general(turned, turned, NT, precision=HIGH, preferred_element_type=F32)
    core = place[4]
    upper = jnp.concatenate([gram[:half, :half], gram[: half // 2, half:]], 0)
    lower = jnp.concatenate([gram[half:, half:], gram[half // 2 : half, half:]], 0)
    gram_mine[...] = jnp.where(core == 0, upper, lower)
    gram_other[...] = jnp.where(core == 0, lower, upper)


def sketch_call(place, count, activations, sketch_matrix):
    rows, width = activations.shape
    columns = sketch_matrix.shape[1]
    packed = (columns // 2 + columns // 4, columns // 2)
    steps = len(DEPTHS)
    smem, anywhere, vmem = (pl.BlockSpec(memory_space=space) for space in (pltpu.SMEM, pltpu.HBM, pltpu.VMEM))
    return pl.pallas_call(
        sketch_kernel,
        out_shape=[
            pltpu.VMEM((rows, width), BF16),
            pltpu.VMEM((rows, columns), F32),
            pltpu.VMEM((2 * columns, rows), BF16),
            pltpu.VMEM(packed, F32),
            pltpu.VMEM(packed, F32),
        ],
        in_specs=[smem, smem, anywhere, anywhere],
        out_specs=[vmem] * 5,
        scratch_shapes=[
            pltpu.VMEM((width, columns), BF16),
            pltpu.SemaphoreType.DMA((steps,)),
            pltpu.SemaphoreType.DMA((steps,)),
        ],
        compiler_params=pltpu.CompilerParams(vmem_limit_bytes=12 * 2**20),
        cost_estimate=pl.CostEstimate(
            flops=2 * rows * width * columns, bytes_accessed=2 * width * (rows + columns), transcendentals=0
        ),
        name="sketch",
    )(place, count, *(pltpu.with_memory_space_constraint(value, pltpu.HBM) for value in (activations, sketch_matrix)))


def projection_kernel(offsets, other, place, split, held, after, *refs):
    columns = split.shape[0] // 2
    core = place[4] + other
    core = jnp.where(core == 2, 0, core)
    for i, (one, two) in enumerate(offsets):
        y = (place[0] + jnp.where(core == 0, two, one)) % SIDE
        x = (place[1] + jnp.where(core == 0, one, two)) % SIDE
        first = pl.multiple_of(((y * SIDE + x) * 2 + core) * WIDE, WIDE)
        both = jnp.dot(split[...], held[:, pl.ds(first, WIDE)], preferred_element_type=F32)
        block = both[:columns] + both[columns:]
        if other:
            refs[0][i] = block
        else:
            block = block + refs[0][i]
            refs[1 + i // SIDE][i % SIDE] = block


def projection_call(place, split, held, after, offsets, other, received=None):
    rows = held.shape[0]
    columns = split.shape[0] // 2
    smem, vmem = (pl.BlockSpec(memory_space=space) for space in (pltpu.SMEM, pltpu.VMEM))
    in_specs = [smem, vmem, vmem, pl.BlockSpec(memory_space=pl.ANY)]
    operands = [place, split, held, after]
    blocks = len(offsets)
    if other:
        out_shape = pltpu.VMEM((blocks, columns, WIDE), F32)
        out_specs = vmem
    else:
        in_specs.append(vmem)
        operands.append(received)
        out_shape = [pltpu.VMEM((SIDE, columns, WIDE), F32)] * (blocks // SIDE)
        out_specs = [vmem] * (blocks // SIDE)
    return pl.pallas_call(
        lambda *refs: projection_kernel(offsets, other, *refs),
        out_shape=out_shape,
        in_specs=in_specs,
        out_specs=out_specs,
        compiler_params=pltpu.CompilerParams(vmem_limit_bytes=8 * 2**20),
        cost_estimate=pl.CostEstimate(
            flops=4 * blocks * rows * WIDE * columns,
            bytes_accessed=blocks * 8 * WIDE * columns,
            transcendentals=0,
        ),
        name="projection",
    )(*operands)


def small_inverse(matrix):
    size = matrix.shape[0]
    groups = [matrix[first : first + GROUP, :] for first in range(0, size, GROUP)]
    lane = lax.broadcasted_iota(jnp.int32, (1, size), 1)
    sublane = lax.broadcasted_iota(jnp.int32, (GROUP, size), 0)
    for at in range(len(groups)):
        first = GROUP * at
        inside = (lane >= first) & (lane < first + GROUP)
        columns = [
            [jnp.broadcast_to(group[:, first + j : first + j + 1], (GROUP, size)) for j in range(GROUP)]
            for group in groups[at:]
        ]
        top = columns[0]
        scaled, done = [], []
        for j in range(GROUP):
            pivot = top[j][j : j + 1, :]
            reciprocal = 1.0 / pivot
            factors = [top[k][j : j + 1, :] * reciprocal for k in range(j + 1, GROUP)]
            for column in columns:
                for k, factor in enumerate(factors, j + 1):
                    column[k] = column[k] - column[j] * factor
            row = jnp.where(inside, 0.0, groups[at][j : j + 1, :])
            for i in range(j):
                row = row - top[i][j : j + 1, :] * scaled[i]
            row = jnp.where(lane == first + j, 1.0, row)
            scaled.append(row * reciprocal)
            done.append(row * lax.rsqrt(pivot))
        for below, column in enumerate(columns[1:], at + 1):
            rest = jnp.where(inside, 0.0, groups[below])
            for j in range(GROUP):
                rest = rest - column[j] * scaled[j]
            groups[below] = rest
        for j in range(GROUP):
            groups[at] = jnp.where(sublane == j, done[j], groups[at])
    rows, cols = (lax.broadcasted_iota(jnp.int32, (size, size), axis) for axis in (0, 1))
    return jnp.where(rows >= cols, jnp.concatenate(groups, 0), 0.0)


def inverse_kernel(place, mine, other, inverse, work):
    size = work.shape[0]
    half = size // 2
    core = place[4]
    upper = jnp.where(core == 0, mine[...], other[...])
    lower = jnp.where(core == 0, other[...], mine[...])
    corner = jnp.concatenate([upper[half:], lower[half:]], 0)
    work[:half, :half] = upper[:half]
    work[:half, half:] = corner
    work[half:, :half] = corner.T
    work[half:, half:] = lower[:half]
    for first in range(0, size, PANEL):
        past = first + PANEL
        rows = pl.ds(first, PANEL)
        block = small_inverse(work[rows, first:past])
        lane = lax.broadcasted_iota(jnp.int32, (PANEL, size), 1)
        parts = [jnp.zeros((PANEL, first), F32)] * (first > 0) + [block]
        parts += [jnp.zeros((PANEL, size - past), F32)] * (past < size)
        placed = jnp.concatenate(parts, 1) if len(parts) > 1 else block
        panel = jnp.dot(block, work[rows, :], precision=HIGH, preferred_element_type=F32)
        panel = jnp.where((lane >= first) & (lane < past), placed, panel)
        inverse[rows, :] = jnp.where(lane < past, panel, 0.0)
        if past < size:
            update = lax.dot_general(panel[:, past:], panel, TN, precision=HIGH, preferred_element_type=F32)
            lane = lax.broadcasted_iota(jnp.int32, (size - past, size), 1)
            old = jnp.where((lane >= first) & (lane < past), 0.0, work[past:, :])
            work[past:, :] = old - update


def vmem_call(kernel, place, operands, out_shape, scratch_shapes, flops, name):
    smem, vmem = (pl.BlockSpec(memory_space=space) for space in (pltpu.SMEM, pltpu.VMEM))
    return pl.pallas_call(
        kernel,
        out_shape=out_shape,
        in_specs=[smem] + [vmem] * len(operands),
        out_specs=jax.tree.map(lambda _: vmem, out_shape),
        scratch_shapes=scratch_shapes,
        compiler_params=pltpu.CompilerParams(vmem_limit_bytes=12 * 2**20),
        cost_estimate=pl.CostEstimate(flops=flops, bytes_accessed=4 * 2**20, transcendentals=0),
        name=name,
    )(place, *operands)


def finish_kernel(scale, place, inverse, mine, other, projected):
    wide = mine.shape[1]
    core = place[4]
    for source, side in ((mine, core), (other, 1 - core)):
        rows = lax.dot_general(source[...].T, inverse[...], NT, precision=HIGH, preferred_element_type=F32)
        projected[pl.ds(pl.multiple_of(side * wide, wide), wide), :] = rows * scale


def on_device(activations, sketch_matrix, row_counts):
    rows_here, width = activations.shape
    columns = sketch_matrix.shape[1]
    square = jax.ShapeDtypeStruct((columns, columns), F32)
    total_rows = rows_here * lax.axis_size(BOTH)
    row, inner = lax.axis_index("rows"), lax.axis_index("inner")
    place = jnp.stack([row >> 2, row & 3, inner >> 1, inner, inner & 1]).astype(jnp.int32)

    held, sketch, split, gram_mine, gram_other = sketch_call(place, row_counts, activations, sketch_matrix)

    first = [(one, two) for one in (1, 3) for two in range(SIDE)]
    second = [(one, two) for one in (2, 0) for two in range(SIDE)]
    first_far = swap_cores(projection_call(place, split, held, place, first, 1))
    packed = gram_mine + swap_cores(gram_other)
    second_far = projection_call(place, split, held, packed, second, 1)
    packed, second_far = add_partner(packed, ("x", "y"), flip, second_far)
    second_far = swap_cores(second_far)
    near = projection_call(place, split, held, packed, first, 0, first_far)
    packed, near = add_partner(packed, ("x", "y"), mirror, near)
    near, packed = lax.optimization_barrier((near, packed))
    one, three = send(near[0], ("x", "y"), 1), send(near[1], ("x", "y"), 3)
    near = projection_call(place, split, held, packed, second, 0, second_far)
    packed, (to_two, mine) = add_partner(packed, ("y", "x"), flip, near)
    two = send(to_two, ("x", "y"), 2)
    packed = add_partner(packed, ("z", "z"), flip)
    packed = add_partner(packed, ("z", "z"), mirror)

    packed = add_partner(packed, ("y", "x"), mirror)
    swapped = swap_cores(packed)

    one, two, three, packed = lax.optimization_barrier((one, two, three, packed))
    blocks = [(mine[j] + two[j]) + (one[j] + three[j]) for j in range(SIDE)]
    arrived = [send(blocks[j], ("y", "x"), j) for j in range(1, SIDE)]
    block = (blocks[0] + arrived[1]) + (arrived[0] + arrived[2])
    packed, swapped, block = lax.optimization_barrier((packed, swapped, block))
    arrived = [send(block, ("z", "z"), s) for s in range(1, SIDE)]
    inverse = vmem_call(
        inverse_kernel, place, (packed, swapped), square, [pltpu.VMEM(square.shape, F32)], 8 * 10**9, "inverse"
    )
    basis = lax.dot_general(sketch, inverse, NT, precision=HIGH) * math.sqrt(total_rows)
    arrived, basis = lax.optimization_barrier((arrived, basis))
    block = (block + arrived[1]) + (arrived[0] + arrived[2])
    projected = vmem_call(
        lambda *refs: finish_kernel(math.sqrt(width / total_rows), *refs), place,
        (inverse, block, swap_cores(block)), jax.ShapeDtypeStruct((2 * WIDE, columns), F32),
        [], 24 * columns**2 * WIDE, "finish",
    )
    return (basis, projected)


def solution(mesh):
    return jax.shard_map(
        on_device,
        mesh=mesh,
        in_specs=(P(("rows", "inner"), None), P(), P(("rows", "inner"))),
        out_specs=(P(("rows", "inner"), None), P("rows", None)),
        check_vma=False,
    )
```

```python
import math

import jax
import jax.numpy as jnp
from jax import lax
from jax.experimental import pallas as pl
from jax.experimental.pallas import tpu as pltpu
from jax.sharding import PartitionSpec as P

SIDE = 4
BOTH = ("rows", "inner")
F32 = jnp.float32
BF16 = jnp.bfloat16
HIGH = lax.Precision.HIGHEST
NT = (((1,), (1,)), ((), ()))
TN = (((0,), (0,)), ((), ()))
GROUP = 8
PANEL = 64
AHEAD = 3
DEPTHS = (512, 1024, 1536, 1536, 1536, 1024, 512, 512)
CHUNK = 128
WIDE = 256


def device(y, x, z, core):
    return ((y % SIDE) * SIDE + x % SIDE) * 2 * SIDE + (z % SIDE) * 2 + core


def pairs(move):
    found = []
    for y in range(SIDE):
        for x in range(SIDE):
            for z in range(SIDE):
                for core in range(2):
                    found.append((device(y, x, z, core), device(*move(y, x, z, core))))
    return found


def step_on(axis, steps, y, x, z, core):
    return (y + steps * (axis == "y"), x + steps * (axis == "x"), z + steps * (axis == "z"), core)


def send(value, axes, steps):
    return lax.ppermute(value, BOTH, pairs(lambda y, x, z, core: step_on(axes[core], steps, y, x, z, core)))


def swap_cores(value):
    return lax.ppermute(value, BOTH, pairs(lambda y, x, z, core: (y, x, z, 1 - core)))


def add_partner(value, axes, partner, beside=None):
    def move(y, x, z, core):
        at = {"y": y, "x": x, "z": z}
        at[axes[core]] = partner(at[axes[core]])
        return (at["y"], at["x"], at["z"], core)

    arrived = lax.ppermute(value, BOTH, pairs(move))
    if beside is None:
        return value + arrived
    arrived, beside = lax.optimization_barrier((arrived, beside))
    return value + arrived, beside


def flip(i):
    return i ^ 1


def mirror(i):
    return SIDE - 1 - i


def sketch_kernel(place, count, act, test, held, sketch, split, gram_mine, gram_other, tests, act_sems, test_sems):
    rows, width = held.shape
    columns = sketch.shape[1]
    half = columns // 2
    copies, parts, first = [], [], 0
    for step, size in enumerate(DEPTHS):
        part = pl.ds(first, size)
        first += size
        parts.append(part)
        copies.append(
            (
                pltpu.make_async_copy(test.at[part, :], tests.at[part, :], test_sems.at[step]),
                pltpu.make_async_copy(act.at[:, part], held.at[:, part], act_sems.at[step]),
            )
        )
    for pair in copies[:AHEAD]:
        for copy in pair:
            copy.start()
    for step, (part, pair) in enumerate(zip(parts, copies)):
        for copy in pair:
            copy.wait()
        for copy in copies[step + AHEAD] if step + AHEAD < len(copies) else ():
            copy.start()
        for first in range(0, rows, CHUNK):
            here = pl.ds(first, CHUNK)
            product = jnp.dot(held[here, part], tests[part, :], preferred_element_type=F32)
            if step == 0:
                sketch[here, :] = product
            else:
                sketch[here, :] += product
    gram = jnp.zeros((columns, columns), F32)
    for first in range(0, rows, 256):
        here = pl.ds(first, 256)
        slots = lax.broadcasted_iota(jnp.int32, (256, columns), 0) + first
        live = jnp.where(slots < count[0], sketch[here, :], 0.0)
        sketch[here, :] = live
        turned = live.T
        high = turned.astype(BF16)
        split[:columns, here] = high
        split[columns:, here] = (turned - high.astype(F32)).astype(BF16)
        gram += lax.dot_general(turned, turned, NT, precision=HIGH, preferred_element_type=F32)
    core = place[4]
    upper = jnp.concatenate([gram[:half, :half], gram[: half // 2, half:]], 0)
    lower = jnp.concatenate([gram[half:, half:], gram[half // 2 : half, half:]], 0)
    gram_mine[...] = jnp.where(core == 0, upper, lower)
    gram_other[...] = jnp.where(core == 0, lower, upper)


def sketch_call(place, count, activations, sketch_matrix):
    rows, width = activations.shape
    columns = sketch_matrix.shape[1]
    packed = (columns // 2 + columns // 4, columns // 2)
    steps = len(DEPTHS)
    smem, anywhere, vmem = (pl.BlockSpec(memory_space=space) for space in (pltpu.SMEM, pltpu.HBM, pltpu.VMEM))
    return pl.pallas_call(
        sketch_kernel,
        out_shape=[
            pltpu.VMEM((rows, width), BF16),
            pltpu.VMEM((rows, columns), F32),
            pltpu.VMEM((2 * columns, rows), BF16),
            pltpu.VMEM(packed, F32),
            pltpu.VMEM(packed, F32),
        ],
        in_specs=[smem, smem, anywhere, anywhere],
        out_specs=[vmem] * 5,
        scratch_shapes=[
            pltpu.VMEM((width, columns), BF16),
            pltpu.SemaphoreType.DMA((steps,)),
            pltpu.SemaphoreType.DMA((steps,)),
        ],
        compiler_params=pltpu.CompilerParams(vmem_limit_bytes=12 * 2**20),
        cost_estimate=pl.CostEstimate(
            flops=2 * rows * width * columns, bytes_accessed=2 * width * (rows + columns), transcendentals=0
        ),
        name="sketch",
    )(place, count, *(pltpu.with_memory_space_constraint(value, pltpu.HBM) for value in (activations, sketch_matrix)))


def projection_kernel(offsets, other, place, split, held, after, *refs):
    columns = split.shape[0] // 2
    core = place[4] + other
    core = jnp.where(core == 2, 0, core)
    for i, (one, two) in enumerate(offsets):
        y = (place[0] + jnp.where(core == 0, two, one)) % SIDE
        x = (place[1] + jnp.where(core == 0, one, two)) % SIDE
        first = pl.multiple_of(((y * SIDE + x) * 2 + core) * WIDE, WIDE)
        both = jnp.dot(split[...], held[:, pl.ds(first, WIDE)], preferred_element_type=F32)
        block = both[:columns] + both[columns:]
        if other:
            refs[0][i] = block
        else:
            block = block + refs[0][i]
            refs[1 + i // SIDE][i % SIDE] = block


def projection_call(place, split, held, after, offsets, other, received=None):
    rows = held.shape[0]
    columns = split.shape[0] // 2
    smem, vmem = (pl.BlockSpec(memory_space=space) for space in (pltpu.SMEM, pltpu.VMEM))
    in_specs = [smem, vmem, vmem, pl.BlockSpec(memory_space=pl.ANY)]
    operands = [place, split, held, after]
    blocks = len(offsets)
    if other:
        out_shape = pltpu.VMEM((blocks, columns, WIDE), F32)
        out_specs = vmem
    else:
        in_specs.append(vmem)
        operands.append(received)
        out_shape = [pltpu.VMEM((SIDE, columns, WIDE), F32)] * (blocks // SIDE)
        out_specs = [vmem] * (blocks // SIDE)
    return pl.pallas_call(
        lambda *refs: projection_kernel(offsets, other, *refs),
        out_shape=out_shape,
        in_specs=in_specs,
        out_specs=out_specs,
        compiler_params=pltpu.CompilerParams(vmem_limit_bytes=8 * 2**20),
        cost_estimate=pl.CostEstimate(
            flops=4 * blocks * rows * WIDE * columns,
            bytes_accessed=blocks * 8 * WIDE * columns,
            transcendentals=0,
        ),
        name="projection",
    )(*operands)


def small_inverse(matrix):
    size = matrix.shape[0]
    groups = [matrix[first : first + GROUP, :] for first in range(0, size, GROUP)]
    lane = lax.broadcasted_iota(jnp.int32, (1, size), 1)
    sublane = lax.broadcasted_iota(jnp.int32, (GROUP, size), 0)
    for at in range(len(groups)):
        first = GROUP * at
        inside = (lane >= first) & (lane < first + GROUP)
        columns = [
            [jnp.broadcast_to(group[:, first + j : first + j + 1], (GROUP, size)) for j in range(GROUP)]
            for group in groups[at:]
        ]
        top = columns[0]
        scaled, done = [], []
        for j in range(GROUP):
            pivot = top[j][j : j + 1, :]
            reciprocal = 1.0 / pivot
            factors = [top[k][j : j + 1, :] * reciprocal for k in range(j + 1, GROUP)]
            for column in columns:
                for k, factor in enumerate(factors, j + 1):
                    column[k] = column[k] - column[j] * factor
            row = jnp.where(inside, 0.0, groups[at][j : j + 1, :])
            for i in range(j):
                row = row - top[i][j : j + 1, :] * scaled[i]
            row = jnp.where(lane == first + j, 1.0, row)
            scaled.append(row * reciprocal)
            done.append(row * lax.rsqrt(pivot))
        for below, column in enumerate(columns[1:], at + 1):
            rest = jnp.where(inside, 0.0, groups[below])
            for j in range(GROUP):
                rest = rest - column[j] * scaled[j]
            groups[below] = rest
        for j in range(GROUP):
            groups[at] = jnp.where(sublane == j, done[j], groups[at])
    rows, cols = (lax.broadcasted_iota(jnp.int32, (size, size), axis) for axis in (0, 1))
    return jnp.where(rows >= cols, jnp.concatenate(groups, 0), 0.0)


def inverse_kernel(place, mine, other, inverse, work):
    size = work.shape[0]
    half = size // 2
    core = place[4]
    upper = jnp.where(core == 0, mine[...], other[...])
    lower = jnp.where(core == 0, other[...], mine[...])
    corner = jnp.concatenate([upper[half:], lower[half:]], 0)
    work[:half, :half] = upper[:half]
    work[:half, half:] = corner
    work[half:, :half] = corner.T
    work[half:, half:] = lower[:half]
    for first in range(0, size, PANEL):
        past = first + PANEL
        rows = pl.ds(first, PANEL)
        block = small_inverse(work[rows, first:past])
        lane = lax.broadcasted_iota(jnp.int32, (PANEL, size), 1)
        parts = [jnp.zeros((PANEL, first), F32)] * (first > 0) + [block]
        parts += [jnp.zeros((PANEL, size - past), F32)] * (past < size)
        placed = jnp.concatenate(parts, 1) if len(parts) > 1 else block
        panel = jnp.dot(block, work[rows, :], precision=HIGH, preferred_element_type=F32)
        panel = jnp.where((lane >= first) & (lane < past), placed, panel)
        inverse[rows, :] = jnp.where(lane < past, panel, 0.0)
        if past < size:
            update = lax.dot_general(panel[:, past:], panel, TN, precision=HIGH, preferred_element_type=F32)
            lane = lax.broadcasted_iota(jnp.int32, (size - past, size), 1)
            old = jnp.where((lane >= first) & (lane < past), 0.0, work[past:, :])
            work[past:, :] = old - update


def vmem_call(kernel, place, operands, out_shape, scratch_shapes, flops, name):
    smem, vmem = (pl.BlockSpec(memory_space=space) for space in (pltpu.SMEM, pltpu.VMEM))
    return pl.pallas_call(
        kernel,
        out_shape=out_shape,
        in_specs=[smem] + [vmem] * len(operands),
        out_specs=jax.tree.map(lambda _: vmem, out_shape),
        scratch_shapes=scratch_shapes,
        compiler_params=pltpu.CompilerParams(vmem_limit_bytes=12 * 2**20),
        cost_estimate=pl.CostEstimate(flops=flops, bytes_accessed=4 * 2**20, transcendentals=0),
        name=name,
    )(place, *operands)


def finish_kernel(scale, place, inverse, mine, other, projected):
    wide = mine.shape[1]
    core = place[4]
    for source, side in ((mine, core), (other, 1 - core)):
        rows = lax.dot_general(source[...].T, inverse[...], NT, precision=HIGH, preferred_element_type=F32)
        projected[pl.ds(pl.multiple_of(side * wide, wide), wide), :] = rows * scale


def on_device(activations, sketch_matrix, row_counts):
    rows_here, width = activations.shape
    columns = sketch_matrix.shape[1]
    square = jax.ShapeDtypeStruct((columns, columns), F32)
    total_rows = rows_here * lax.axis_size(BOTH)
    row, inner = lax.axis_index("rows"), lax.axis_index("inner")
    place = jnp.stack([row >> 2, row & 3, inner >> 1, inner, inner & 1]).astype(jnp.int32)

    held, sketch, split, gram_mine, gram_other = sketch_call(place, row_counts, activations, sketch_matrix)

    first = [(one, two) for one in (2, 0) for two in range(SIDE)]
    second = [(one, two) for one in (1, 3) for two in range(SIDE)]
    first_far = swap_cores(projection_call(place, split, held, place, first, 1))
    packed = gram_mine + swap_cores(gram_other)
    second_far = projection_call(place, split, held, packed, second, 1)
    packed, second_far = add_partner(packed, ("x", "y"), flip, second_far)
    second_far = swap_cores(second_far)
    near = projection_call(place, split, held, packed, first, 0, first_far)
    packed, near = add_partner(packed, ("x", "y"), mirror, near)
    near, packed = lax.optimization_barrier((near, packed))
    two, mine = send(near[0], ("x", "y"), 2), near[1]
    near = projection_call(place, split, held, packed, second, 0, second_far)
    packed, (to_one, to_three) = add_partner(packed, ("y", "x"), flip, near)
    one, three = send(to_one, ("x", "y"), 1), send(to_three, ("x", "y"), 3)
    packed = add_partner(packed, ("z", "z"), flip)
    packed = add_partner(packed, ("z", "z"), mirror)

    packed = add_partner(packed, ("y", "x"), mirror)
    swapped = swap_cores(packed)

    one, two, three, packed = lax.optimization_barrier((one, two, three, packed))
    blocks = [(mine[j] + two[j]) + (one[j] + three[j]) for j in range(SIDE)]
    two, three, one = (send(blocks[j], ("y", "x"), j) for j in (2, 3, 1))
    block = (blocks[0] + two) + (one + three)
    packed, swapped, block = lax.optimization_barrier((packed, swapped, block))
    arrived = [send(block, ("z", "z"), s) for s in (2, 3, 1)]
    inverse = vmem_call(
        inverse_kernel, place, (packed, swapped), square, [pltpu.VMEM(square.shape, F32)], 8 * 10**9, "inverse"
    )
    basis = lax.dot_general(sketch, inverse, NT, precision=HIGH) * math.sqrt(total_rows)
    arrived, basis = lax.optimization_barrier((arrived, basis))
    block = (block + arrived[0]) + (arrived[1] + arrived[2])
    projected = vmem_call(
        lambda *refs: finish_kernel(math.sqrt(width / total_rows), *refs), place,
        (inverse, block, swap_cores(block)), jax.ShapeDtypeStruct((2 * WIDE, columns), F32),
        [], 24 * columns**2 * WIDE, "finish",
    )
    return (basis, projected)


def solution(mesh):
    return jax.shard_map(
        on_device,
        mesh=mesh,
        in_specs=(P(("rows", "inner"), None), P(), P(("rows", "inner"))),
        out_specs=(P(("rows", "inner"), None), P("rows", None)),
        check_vma=False,
    )
```

```python
import math

import jax
import jax.numpy as jnp
from jax import lax
from jax.experimental import pallas as pl
from jax.experimental.pallas import tpu as pltpu
from jax.sharding import PartitionSpec as P

SIDE = 4
BOTH = ("rows", "inner")
F32 = jnp.float32
BF16 = jnp.bfloat16
HIGH = lax.Precision.HIGHEST
NT = (((1,), (1,)), ((), ()))
TN = (((0,), (0,)), ((), ()))
GROUP = 8
PANEL = 64
AHEAD = 3
DEPTHS = (512, 1024, 1536, 1536, 1536, 1024, 512, 512)
CHUNK = 128
WIDE = 256


def device(y, x, z, core):
    return ((y % SIDE) * SIDE + x % SIDE) * 2 * SIDE + (z % SIDE) * 2 + core


def pairs(move):
    found = []
    for y in range(SIDE):
        for x in range(SIDE):
            for z in range(SIDE):
                for core in range(2):
                    found.append((device(y, x, z, core), device(*move(y, x, z, core))))
    return found


def step_on(axis, steps, y, x, z, core):
    return (y + steps * (axis == "y"), x + steps * (axis == "x"), z + steps * (axis == "z"), core)


def send(value, axes, steps):
    return lax.ppermute(value, BOTH, pairs(lambda y, x, z, core: step_on(axes[core], steps, y, x, z, core)))


def swap_cores(value):
    return lax.ppermute(value, BOTH, pairs(lambda y, x, z, core: (y, x, z, 1 - core)))


def add_partner(value, axes, partner, beside=None):
    def move(y, x, z, core):
        at = {"y": y, "x": x, "z": z}
        at[axes[core]] = partner(at[axes[core]])
        return (at["y"], at["x"], at["z"], core)

    arrived = lax.ppermute(value, BOTH, pairs(move))
    if beside is None:
        return value + arrived
    arrived, beside = lax.optimization_barrier((arrived, beside))
    return value + arrived, beside


def flip(i):
    return i ^ 1


def mirror(i):
    return SIDE - 1 - i


def sketch_kernel(place, count, act, test, held, sketch, split, gram_mine, gram_other, tests, act_sems, test_sems):
    rows, width = held.shape
    columns = sketch.shape[1]
    half = columns // 2
    copies, parts, first = [], [], 0
    for step, size in enumerate(DEPTHS):
        part = pl.ds(first, size)
        first += size
        parts.append(part)
        copies.append(
            (
                pltpu.make_async_copy(test.at[part, :], tests.at[part, :], test_sems.at[step]),
                pltpu.make_async_copy(act.at[:, part], held.at[:, part], act_sems.at[step]),
            )
        )
    for pair in copies[:AHEAD]:
        for copy in pair:
            copy.start()
    for step, (part, pair) in enumerate(zip(parts, copies)):
        for copy in pair:
            copy.wait()
        for copy in copies[step + AHEAD] if step + AHEAD < len(copies) else ():
            copy.start()
        for first in range(0, rows, CHUNK):
            here = pl.ds(first, CHUNK)
            product = jnp.dot(held[here, part], tests[part, :], preferred_element_type=F32)
            if step == 0:
                sketch[here, :] = product
            else:
                sketch[here, :] += product
    gram = jnp.zeros((columns, columns), F32)
    for first in range(0, rows, 256):
        here = pl.ds(first, 256)
        slots = lax.broadcasted_iota(jnp.int32, (256, columns), 0) + first
        live = jnp.where(slots < count[0], sketch[here, :], 0.0)
        sketch[here, :] = live
        turned = live.T
        high = turned.astype(BF16)
        split[:columns, here] = high
        split[columns:, here] = (turned - high.astype(F32)).astype(BF16)
        gram += lax.dot_general(turned, turned, NT, precision=HIGH, preferred_element_type=F32)
    core = place[4]
    upper = jnp.concatenate([gram[:half, :half], gram[: half // 2, half:]], 0)
    lower = jnp.concatenate([gram[half:, half:], gram[half // 2 : half, half:]], 0)
    gram_mine[...] = jnp.where(core == 0, upper, lower)
    gram_other[...] = jnp.where(core == 0, lower, upper)


def sketch_call(place, count, activations, sketch_matrix):
    rows, width = activations.shape
    columns = sketch_matrix.shape[1]
    packed = (columns // 2 + columns // 4, columns // 2)
    steps = len(DEPTHS)
    smem, anywhere, vmem = (pl.BlockSpec(memory_space=space) for space in (pltpu.SMEM, pltpu.HBM, pltpu.VMEM))
    return pl.pallas_call(
        sketch_kernel,
        out_shape=[
            pltpu.VMEM((rows, width), BF16),
            pltpu.VMEM((rows, columns), F32),
            pltpu.VMEM((2 * columns, rows), BF16),
            pltpu.VMEM(packed, F32),
            pltpu.VMEM(packed, F32),
        ],
        in_specs=[smem, smem, anywhere, anywhere],
        out_specs=[vmem] * 5,
        scratch_shapes=[
            pltpu.VMEM((width, columns), BF16),
            pltpu.SemaphoreType.DMA((steps,)),
            pltpu.SemaphoreType.DMA((steps,)),
        ],
        compiler_params=pltpu.CompilerParams(vmem_limit_bytes=12 * 2**20),
        cost_estimate=pl.CostEstimate(
            flops=2 * rows * width * columns, bytes_accessed=2 * width * (rows + columns), transcendentals=0
        ),
        name="sketch",
    )(place, count, *(pltpu.with_memory_space_constraint(value, pltpu.HBM) for value in (activations, sketch_matrix)))


def projection_kernel(offsets, other, place, split, held, after, *refs):
    columns = split.shape[0] // 2
    core = place[4] + other
    core = jnp.where(core == 2, 0, core)
    for i, (one, two) in enumerate(offsets):
        y = (place[0] + jnp.where(core == 0, two, one)) % SIDE
        x = (place[1] + jnp.where(core == 0, one, two)) % SIDE
        first = pl.multiple_of(((y * SIDE + x) * 2 + core) * WIDE, WIDE)
        both = jnp.dot(split[...], held[:, pl.ds(first, WIDE)], preferred_element_type=F32)
        block = both[:columns] + both[columns:]
        if other:
            refs[0][i] = block
        else:
            block = block + refs[0][i]
            refs[1 + i // SIDE][i % SIDE] = block


def projection_call(place, split, held, after, offsets, other, received=None):
    rows = held.shape[0]
    columns = split.shape[0] // 2
    smem, vmem = (pl.BlockSpec(memory_space=space) for space in (pltpu.SMEM, pltpu.VMEM))
    in_specs = [smem, vmem, vmem, pl.BlockSpec(memory_space=pl.ANY)]
    operands = [place, split, held, after]
    blocks = len(offsets)
    if other:
        out_shape = pltpu.VMEM((blocks, columns, WIDE), F32)
        out_specs = vmem
    else:
        in_specs.append(vmem)
        operands.append(received)
        out_shape = [pltpu.VMEM((SIDE, columns, WIDE), F32)] * (blocks // SIDE)
        out_specs = [vmem] * (blocks // SIDE)
    return pl.pallas_call(
        lambda *refs: projection_kernel(offsets, other, *refs),
        out_shape=out_shape,
        in_specs=in_specs,
        out_specs=out_specs,
        compiler_params=pltpu.CompilerParams(vmem_limit_bytes=8 * 2**20),
        cost_estimate=pl.CostEstimate(
            flops=4 * blocks * rows * WIDE * columns,
            bytes_accessed=blocks * 8 * WIDE * columns,
            transcendentals=0,
        ),
        name="projection",
    )(*operands)


def small_inverse(matrix):
    size = matrix.shape[0]
    groups = [matrix[first : first + GROUP, :] for first in range(0, size, GROUP)]
    lane = lax.broadcasted_iota(jnp.int32, (1, size), 1)
    sublane = lax.broadcasted_iota(jnp.int32, (GROUP, size), 0)
    for at in range(len(groups)):
        first = GROUP * at
        inside = (lane >= first) & (lane < first + GROUP)
        columns = [
            [jnp.broadcast_to(group[:, first + j : first + j + 1], (GROUP, size)) for j in range(GROUP)]
            for group in groups[at:]
        ]
        top = columns[0]
        scaled, done = [], []
        for j in range(GROUP):
            pivot = top[j][j : j + 1, :]
            reciprocal = 1.0 / pivot
            factors = [top[k][j : j + 1, :] * reciprocal for k in range(j + 1, GROUP)]
            for column in columns:
                for k, factor in enumerate(factors, j + 1):
                    column[k] = column[k] - column[j] * factor
            row = jnp.where(inside, 0.0, groups[at][j : j + 1, :])
            for i in range(j):
                row = row - top[i][j : j + 1, :] * scaled[i]
            row = jnp.where(lane == first + j, 1.0, row)
            scaled.append(row * reciprocal)
            done.append(row * lax.rsqrt(pivot))
        for below, column in enumerate(columns[1:], at + 1):
            rest = jnp.where(inside, 0.0, groups[below])
            for j in range(GROUP):
                rest = rest - column[j] * scaled[j]
            groups[below] = rest
        for j in range(GROUP):
            groups[at] = jnp.where(sublane == j, done[j], groups[at])
    rows, cols = (lax.broadcasted_iota(jnp.int32, (size, size), axis) for axis in (0, 1))
    return jnp.where(rows >= cols, jnp.concatenate(groups, 0), 0.0)


def inverse_kernel(place, mine, other, inverse, work):
    size = work.shape[0]
    half = size // 2
    core = place[4]
    upper = jnp.where(core == 0, mine[...], other[...])
    lower = jnp.where(core == 0, other[...], mine[...])
    corner = jnp.concatenate([upper[half:], lower[half:]], 0)
    work[:half, :half] = upper[:half]
    work[:half, half:] = corner
    work[half:, :half] = corner.T
    work[half:, half:] = lower[:half]
    for first in range(0, size, PANEL):
        past = first + PANEL
        rows = pl.ds(first, PANEL)
        block = small_inverse(work[rows, first:past])
        lane = lax.broadcasted_iota(jnp.int32, (PANEL, size), 1)
        parts = [jnp.zeros((PANEL, first), F32)] * (first > 0) + [block]
        parts += [jnp.zeros((PANEL, size - past), F32)] * (past < size)
        placed = jnp.concatenate(parts, 1) if len(parts) > 1 else block
        panel = jnp.dot(block, work[rows, :], precision=HIGH, preferred_element_type=F32)
        panel = jnp.where((lane >= first) & (lane < past), placed, panel)
        inverse[rows, :] = jnp.where(lane < past, panel, 0.0)
        if past < size:
            update = lax.dot_general(panel[:, past:], panel, TN, precision=HIGH, preferred_element_type=F32)
            lane = lax.broadcasted_iota(jnp.int32, (size - past, size), 1)
            old = jnp.where((lane >= first) & (lane < past), 0.0, work[past:, :])
            work[past:, :] = old - update


def vmem_call(kernel, place, operands, out_shape, scratch_shapes, flops, name):
    smem, vmem = (pl.BlockSpec(memory_space=space) for space in (pltpu.SMEM, pltpu.VMEM))
    return pl.pallas_call(
        kernel,
        out_shape=out_shape,
        in_specs=[smem] + [vmem] * len(operands),
        out_specs=jax.tree.map(lambda _: vmem, out_shape),
        scratch_shapes=scratch_shapes,
        compiler_params=pltpu.CompilerParams(vmem_limit_bytes=12 * 2**20),
        cost_estimate=pl.CostEstimate(flops=flops, bytes_accessed=4 * 2**20, transcendentals=0),
        name=name,
    )(place, *operands)


def finish_kernel(scale, place, inverse, block, mine, projected):
    wide = block.shape[1]
    core = place[4]
    rows = lax.dot_general(block[...].T, inverse[...], NT, precision=HIGH, preferred_element_type=F32)
    projected[pl.ds(pl.multiple_of(core * wide, wide), wide), :] = mine[...]
    projected[pl.ds(pl.multiple_of((1 - core) * wide, wide), wide), :] = rows * scale


def finish_mine(scale, place, inverse, block, rows):
    rows[...] = scale * lax.dot_general(
        block[...].T, inverse[...], NT, precision=HIGH, preferred_element_type=F32
    )


def on_device(activations, sketch_matrix, row_counts):
    rows_here, width = activations.shape
    columns = sketch_matrix.shape[1]
    square = jax.ShapeDtypeStruct((columns, columns), F32)
    total_rows = rows_here * lax.axis_size(BOTH)
    row, inner = lax.axis_index("rows"), lax.axis_index("inner")
    place = jnp.stack([row >> 2, row & 3, inner >> 1, inner, inner & 1]).astype(jnp.int32)

    held, sketch, split, gram_mine, gram_other = sketch_call(place, row_counts, activations, sketch_matrix)

    first = [(one, two) for one in (2, 0) for two in range(SIDE)]
    second = [(one, two) for one in (1, 3) for two in range(SIDE)]
    first_far = swap_cores(projection_call(place, split, held, place, first, 1))
    packed = gram_mine + swap_cores(gram_other)
    second_far = projection_call(place, split, held, packed, second, 1)
    packed, second_far = add_partner(packed, ("x", "y"), flip, second_far)
    second_far = swap_cores(second_far)
    near = projection_call(place, split, held, packed, first, 0, first_far)
    packed, near = add_partner(packed, ("x", "y"), mirror, near)
    near, packed = lax.optimization_barrier((near, packed))
    two, mine = send(near[0], ("x", "y"), 2), near[1]
    near = projection_call(place, split, held, packed, second, 0, second_far)
    packed, (to_one, to_three) = add_partner(packed, ("y", "x"), flip, near)
    one, three = send(to_one, ("x", "y"), 1), send(to_three, ("x", "y"), 3)
    packed = add_partner(packed, ("z", "z"), flip)
    packed = add_partner(packed, ("z", "z"), mirror)

    packed = add_partner(packed, ("y", "x"), mirror)
    swapped = swap_cores(packed)

    one, two, three, packed = lax.optimization_barrier((one, two, three, packed))
    blocks = [(mine[j] + two[j]) + (one[j] + three[j]) for j in range(SIDE)]
    two, three, one = (send(blocks[j], ("y", "x"), j) for j in (2, 3, 1))
    block = (blocks[0] + two) + (one + three)
    packed, swapped, block = lax.optimization_barrier((packed, swapped, block))
    arrived = [send(block, ("z", "z"), s) for s in (2, 3, 1)]
    inverse = vmem_call(
        inverse_kernel, place, (packed, swapped), square, [pltpu.VMEM(square.shape, F32)], 8 * 10**9, "inverse"
    )
    basis = lax.dot_general(sketch, inverse, NT, precision=HIGH) * math.sqrt(total_rows)
    arrived, basis = lax.optimization_barrier((arrived, basis))
    block = (block + arrived[0]) + (arrived[1] + arrived[2])
    scale = math.sqrt(width / total_rows)
    other = swap_cores(block)
    rows = vmem_call(
        lambda *refs: finish_mine(scale, *refs), place, (inverse, block), square, [], 10**9, "finish_mine"
    )
    other, rows = lax.optimization_barrier((other, rows))
    projected = vmem_call(
        lambda *refs: finish_kernel(scale, *refs), place, (inverse, other, rows),
        jax.ShapeDtypeStruct((2 * WIDE, columns), F32), [], 10**9, "finish",
    )
    return (basis, projected)


def solution(mesh):
    return jax.shard_map(
        on_device,
        mesh=mesh,
        in_specs=(P(("rows", "inner"), None), P(), P(("rows", "inner"))),
        out_specs=(P(("rows", "inner"), None), P("rows", None)),
        check_vma=False,
    )
```
